256 devices in a mesh: face: 8 (over x_hi, y), slab: 32 (over x_lo, z, core).
Axes of the slice: x: 4 (x_hi: 2, x_lo: 2; x = x_hi * 2 + x_lo), y: 4, z: 8, core: 2. Of those that a mesh axis runs over, the one named last changes fastest.
Arguments:
- activations: bfloat16 [8, 256, 512, 128], P('face', 'slab'), may hold values from -6 to 6
- cotangent: bfloat16 [8, 256, 512, 128], P('face', 'slab'), may hold values from -6 to 6
- conv_weight: float32 [9, 128], replicated, may hold values from -2 to 2
- norm_gain: float32 [128], replicated, may hold values from 0.1 to 1.9
- w_in: bfloat16 [128, 512], replicated, may hold values from -0.5 to 0.5
- w_out: bfloat16 [512, 128], replicated, may hold values from -0.25 to 0.25
- layer_scale: float32 [128], replicated, may hold values from 0.25 to 2
- neighbours: int32 [8, 32, 2, 4], P('face', 'slab'), may hold values from 0 to 31, as said below
Outputs:
- input_gradient: bfloat16 [8, 256, 512, 128], P('face', 'slab')
- conv_grad: float32 [9, 128], replicated
- gain_grad: float32 [128], replicated
- in_grad: float32 [128, 512], replicated
- out_grad: float32 [512, 128], replicated
- scale_grad: float32 [128], replicated
The draws below stay inside these ranges and needn't reach their ends.
Inputs may be any that keep to these rules, and one draw needn't show every extreme that they name: `neighbours`: entry [f, s, e] = (source face, source slab, source edge, code). Side edges of the 8 faces are joined in pairs, never an edge with itself; both edges of a pair name each other with the same code. For one face and edge all slabs have the same source face, edge and code; the source slab is s for code 0 and 31 - s for code 1.
All inputs are finite; a program needn't handle non-finite values.
Results may differ from the reference program's by a relative error of at most 0.0076.
Values may be sent and summed in bfloat16 or wider, within the bound.
A program may use at most 128 MiB of HBM per device.

```python
import math
from functools import partial
import jax
import jax.numpy as jnp
from jax import lax

CHANNEL_COUNT = 128
HID = 512
DEVICE_ROWS = 8
FACE_COLUMNS = 512
DILATION_STEP = 2
FACES = 8
SLABS = 32
FACE_ROWS = 256
CELLS = 1048576


def draw_neighbours(key, part):
    key = jax.random.fold_in(key, 11)
    order_key, code_key = jax.random.split(key)
    order = jax.random.permutation(order_key, 2 * FACES)
    firsts = order[0::2]
    seconds = order[1::2]
    partner = jnp.zeros((2 * FACES,), jnp.int32).at[firsts].set(seconds).at[seconds].set(firsts)
    pair_code = jax.random.randint(code_key, (FACES,), 0, 2).astype(jnp.int32)
    codes = jnp.zeros((2 * FACES,), jnp.int32).at[firsts].set(pair_code).at[seconds].set(pair_code)
    src_face = (partner // 2).reshape(FACES, 1, 2)
    src_edge = (partner % 2).reshape(FACES, 1, 2)
    rotation = codes.reshape(FACES, 1, 2)
    slab_ids = jnp.arange(SLABS, dtype=jnp.int32).reshape(1, SLABS, 1)
    src_slab = jnp.where(rotation == 1, SLABS - 1 - slab_ids, slab_ids)
    array_dimensions = (FACES, SLABS, 2)
    return jnp.stack([jnp.broadcast_to(src_face, array_dimensions), jnp.broadcast_to(src_slab, array_dimensions), jnp.broadcast_to(src_edge, array_dimensions), jnp.broadcast_to(rotation, array_dimensions)], -1).astype(jnp.int32)


def steps_of(key, shape, cuts, low, high):
    def one(dim, blocks):
        draws = jax.random.uniform(jax.random.fold_in(jax.random.fold_in(key, 6), dim), (blocks,), jnp.float32, low / len(cuts), high / len(cuts))
        return jnp.repeat(jnp.exp(draws), shape[dim] // blocks).reshape((-1,) + (1,) * (len(shape) - dim - 1))

    level = one(*cuts[0])
    for cut in cuts[1:]:
        level = level * one(*cut)
    return level


def scatter_about(key, shape, deviation, most, pieces=(), kind=jnp.bfloat16):
    values = deviation * jax.random.normal(key, shape, jnp.float32)
    if pieces:
        values = values * steps_of(key, shape, pieces, -0.22, 0.18)
    return jnp.clip(values, -most, most).astype(kind)


def setup_inputs(seed: int = 0) -> dict:
    key_of = jax.random.split(jax.random.key(seed), 9)
    activations = scatter_about(key_of[0], (FACES, FACE_ROWS, FACE_COLUMNS, CHANNEL_COUNT), 1.0, 6.0, ((0, 8), (1, 32)))
    cotangent = scatter_about(key_of[1], (FACES, FACE_ROWS, FACE_COLUMNS, CHANNEL_COUNT), 1.0, 6.0, ((0, 8), (1, 32)))
    conv_weight = scatter_about(key_of[2], (9, CHANNEL_COUNT), 9 ** -0.5, 2.0, (), jnp.float32)
    norm_gain = jnp.clip(1.0 + 0.18 * jax.random.normal(key_of[3], (CHANNEL_COUNT,), jnp.float32), 0.1, 1.9)
    w_in = scatter_about(key_of[4], (CHANNEL_COUNT, HID), CHANNEL_COUNT ** -0.5, 0.5)
    w_out = scatter_about(key_of[5], (HID, CHANNEL_COUNT), HID ** -0.5, 0.25)
    layer_scale = jnp.clip(jnp.exp(jax.random.uniform(key_of[6], (CHANNEL_COUNT,), jnp.float32, math.log(0.25), math.log(2.0))), 0.25, 2.0)
    neighbours = draw_neighbours(jax.random.fold_in(key_of[8], 71), 0)
    return {"activations": activations, "cotangent": cotangent, "conv_weight": conv_weight, "norm_gain": norm_gain, "w_in": w_in, "w_out": w_out, "layer_scale": layer_scale, "neighbours": neighbours}


EPSILON = 1e-06

def dilated(weights, padded_input):
    row_total = padded_input.shape[0] - 2 * DILATION_STEP
    column_total = padded_input.shape[1] - 2 * DILATION_STEP
    accumulated = jnp.zeros((row_total, column_total, padded_input.shape[2]), jnp.float32)
    for row_offset in range(3):
        for column_offset in range(3):
            sliding_view = padded_input[row_offset * DILATION_STEP:row_offset * DILATION_STEP + row_total, column_offset * DILATION_STEP:column_offset * DILATION_STEP + column_total]
            accumulated = accumulated + weights[3 * row_offset + column_offset] * sliding_view
    return accumulated

def norm_backward(upstream, normed, inverse):
    return inverse * (upstream - lax.optimization_barrier(jnp.mean(upstream, -1, keepdims=True)) - normed * lax.optimization_barrier(jnp.mean(upstream * normed, -1, keepdims=True)))

def mlp_pass(conv_out, upstream, norm_gain, w_in, w_out, layer_scale):
    channels = conv_out.shape[-1]
    features = conv_out.reshape(-1, channels)
    average = lax.optimization_barrier(jnp.mean(features, -1, keepdims=True))
    centred = features - average
    variance = lax.optimization_barrier(jnp.mean(centred * centred, -1, keepdims=True))
    inverse = lax.rsqrt(variance + EPSILON)
    normed = centred * inverse
    scaled = (normed * norm_gain).astype(jnp.bfloat16)
    hidden = jnp.dot(scaled, w_in, preferred_element_type=jnp.float32)
    activated, gelu_back = jax.vjp(partial(jax.nn.gelu, approximate=False), hidden)
    activated_b = activated.astype(jnp.bfloat16)
    mixed = jnp.dot(activated_b, w_out, preferred_element_type=jnp.float32)
    cotan = upstream.reshape(-1, channels).astype(jnp.float32)
    scale_grad = lax.optimization_barrier(jnp.sum(cotan * mixed, 0))
    branch = (cotan * layer_scale).astype(jnp.bfloat16)
    out_grad = jnp.dot(activated_b.T, branch, preferred_element_type=jnp.float32)
    hidden_grad = gelu_back(jnp.dot(branch, w_out.T, preferred_element_type=jnp.float32))[0].astype(jnp.bfloat16)
    in_grad = jnp.dot(scaled.T, hidden_grad, preferred_element_type=jnp.float32)
    normed_grad = jnp.dot(hidden_grad, w_in.T, preferred_element_type=jnp.float32)
    gain_grad = lax.optimization_barrier(jnp.sum(normed_grad * normed, 0))
    conv_grad_b = norm_backward(normed_grad * norm_gain, normed, inverse).astype(jnp.bfloat16)
    return (conv_grad_b.reshape(conv_out.shape), (gain_grad, in_grad, out_grad, scale_grad))

def reference(activations, cotangent, conv_weight, norm_gain, w_in, w_out, layer_scale, neighbours):
    face_total = activations.shape[0]
    slab_total = neighbours.shape[1]
    source_face = neighbours[..., 0]
    source_slab = neighbours[..., 1]
    source_edge = neighbours[..., 2]
    rotation = neighbours[..., 3]
    bands_list = jnp.stack([activations[:, :, :DILATION_STEP], jnp.flip(activations[:, :, FACE_COLUMNS - DILATION_STEP:], 2)], 1)
    bands_list = bands_list.reshape(face_total, 2, slab_total, DEVICE_ROWS, DILATION_STEP, CHANNEL_COUNT)
    fragments = bands_list[source_face, source_edge, source_slab]
    flipped = rotation[..., None, None, None] == 1
    fragments = jnp.where(flipped, jnp.flip(fragments, 3), fragments)
    left_band = fragments[:, :, 0].reshape(face_total, FACE_ROWS, DILATION_STEP, CHANNEL_COUNT)
    right_band = fragments[:, :, 1].reshape(face_total, FACE_ROWS, DILATION_STEP, CHANNEL_COUNT)
    widened = jnp.concatenate([jnp.flip(left_band, 2), activations, right_band], 2)

    def face_step(carry, inputs):
        face_broadened, face_up = inputs
        padded_input = jnp.pad(face_broadened.astype(jnp.float32), ((DILATION_STEP, DILATION_STEP), (0, 0), (0, 0)))
        conv_out, conv_back = jax.vjp(dilated, conv_weight, padded_input)
        conv_grad_b, mlp_grads = mlp_pass(conv_out, face_up, norm_gain, w_in, w_out, layer_scale)
        tap_grad, padded_gradient = conv_back(conv_grad_b.astype(jnp.float32))
        next_carried = (carry[0] + tap_grad,) + tuple((old + extra for old, extra in zip(carry[1:], mlp_grads)))
        return (next_carried, padded_gradient[DILATION_STEP:DILATION_STEP + FACE_ROWS])
    start = (jnp.zeros((9, CHANNEL_COUNT), jnp.float32), jnp.zeros((CHANNEL_COUNT,), jnp.float32), jnp.zeros((CHANNEL_COUNT, HID), jnp.float32), jnp.zeros((HID, CHANNEL_COUNT), jnp.float32), jnp.zeros((CHANNEL_COUNT,), jnp.float32))
    sums, broadened_gradient = lax.scan(face_step, start, (widened, cotangent))
    left_junction = jnp.flip(broadened_gradient[:, :, :DILATION_STEP], 2).reshape(face_total, slab_total, DEVICE_ROWS, DILATION_STEP, CHANNEL_COUNT)
    right_junction = broadened_gradient[:, :, FACE_COLUMNS + DILATION_STEP:].reshape(face_total, slab_total, DEVICE_ROWS, DILATION_STEP, CHANNEL_COUNT)
    returned = jnp.stack([left_junction, right_junction], 2)
    returned = jnp.where(flipped, jnp.flip(returned, 3), returned)
    collected_rows = jnp.zeros((face_total, 2, slab_total, DEVICE_ROWS, DILATION_STEP, CHANNEL_COUNT), jnp.float32)
    collected_rows = collected_rows.at[source_face, source_edge, source_slab].add(returned)
    collected_rows = collected_rows.reshape(face_total, 2, FACE_ROWS, DILATION_STEP, CHANNEL_COUNT)
    input_gradient = cotangent.astype(jnp.float32) + broadened_gradient[:, :, DILATION_STEP:FACE_COLUMNS + DILATION_STEP]
    input_gradient = input_gradient.at[:, :, :DILATION_STEP].add(collected_rows[:, 0])
    input_gradient = input_gradient.at[:, :, FACE_COLUMNS - DILATION_STEP:].add(jnp.flip(collected_rows[:, 1], 2))
    factor = float(CELLS) ** (-0.5)
    return (input_gradient.astype(jnp.bfloat16), sums[0] * factor, sums[1] * factor, sums[2] * factor, sums[3] * factor, sums[4] * factor)
```

```python
import math
from functools import partial

import jax
import jax.numpy as jnp
from jax import lax
from jax.experimental import pallas as pl
from jax.experimental.pallas import tpu as pltpu
from jax.sharding import PartitionSpec as P

F32, BF16 = jnp.float32, jnp.bfloat16
FACES, SLABS = 8, 32
DEPTH = 8
PLANE = 32
ROWS, COLS, CH, HID = 8, 512, 128, 512
PAD = 8
WIDE = COLS + 2 * PAD
CHUNK = 128
SHARE = 32
CELLS = FACES * SLABS * ROWS * COLS
FACTOR = float(CELLS) ** (-0.5)
EPSILON = 1e-6
SQRT_HALF = math.sqrt(0.5)
EXPONENT = -math.log2(math.e)
BIAS = math.log2(2 / math.sqrt(2 * math.pi))
MESH = pl.DeviceIdType.MESH


def dot(a, b, dims=((1,), (0,))):
    return lax.dot_general(a, b, (dims, ((), ())), preferred_element_type=F32)


def prepare(wi, wo, gain, scale, wd_ref, wn_ref):
    wd_ref[...] = (wo.astype(F32) * (0.5 * scale)).T.astype(BF16)
    wit = wi.astype(F32).T
    wn_ref[:, :CH] = wit.astype(BF16)
    mean = jnp.mean(wit * gain, -1, keepdims=True)
    wn_ref[:, CH:] = jnp.broadcast_to(mean, (HID, CH)).astype(BF16)


def row_pass(r, cw, gain, xp, cot_ref, wi_ref, wd_ref, wn_ref, sc, nm, iv, hg, ng, gp, gb, og, ig, tg):
    ones = jnp.full((2 * CH, CH), 1 / CH, BF16)
    for c0 in range(0, COLS, CHUNK):
        acc = None
        for i in range(3):
            for j in range(3):
                t = cw[3 * i + j : 3 * i + j + 1] * xp[r + 2 * i, pl.ds(PAD - 2 + 2 * j + c0, CHUNK), :]
                acc = t if acc is None else acc + t
        hi = acc.astype(BF16)
        lo = (acc - hi.astype(F32)).astype(BF16)
        centred = acc - dot(jnp.concatenate([hi, lo], 1), ones)
        variance = dot((centred * centred).astype(BF16), ones[:CH])
        inverse = lax.rsqrt(variance + EPSILON)
        normed = centred * inverse
        sc[c0 : c0 + CHUNK, :] = (normed * gain).astype(BF16)
        nm[c0 : c0 + CHUNK, :] = normed
        iv[c0 : c0 + CHUNK, :] = inverse
    cot = cot_ref[0, r]
    scaled = sc[...]
    for n0 in range(0, HID, 256):
        hidden = dot(scaled, wi_ref[:, n0 : n0 + 256])
        upstream = dot(cot, wd_ref[:, n0 : n0 + 256])
        x = hidden * SQRT_HALF
        twice = 1.0 + lax.erf(x)
        activated = (hidden * twice).astype(BF16)
        density = jnp.exp2(x * x * EXPONENT + BIAS)
        hidden_grad = ((twice + hidden * density) * upstream).astype(BF16)
        hg[:, n0 : n0 + 256] = hidden_grad
        og[:, n0 : n0 + 256] += dot(cot, activated, ((0,), (0,)))
        ig[:, n0 : n0 + 256] += dot(scaled, hidden_grad, ((0,), (0,)))
    ng[...] = dot(hg[...], wn_ref[...])
    for c0 in range(0, COLS, CHUNK):
        d = ng[c0 : c0 + CHUNK, :CH] * gain
        d_mean = ng[c0 : c0 + CHUNK, CH:]
        normed = nm[c0 : c0 + CHUNK, :]
        dn_mean = dot((d * normed).astype(BF16), ones[:CH])
        gb16 = (iv[c0 : c0 + CHUNK, :] * (d - d_mean - normed * dn_mean)).astype(BF16)
        gb[r, c0 : c0 + CHUNK, :] = gb16
        g = gb16.astype(F32)
        gp[r + 2, PAD + c0 : PAD + c0 + CHUNK, :] = g
        for i in range(3):
            for j in range(3):
                t = g * xp[r + 2 * i, pl.ds(PAD - 2 + 2 * j + c0, CHUNK), :]
                tg[3 * i + j] += t.reshape(CHUNK // 8, 8, CH).sum(0)


def transposed_row(r, cw, gp, cot_ref, dx, edge):
    for c0 in range(0, COLS, CHUNK):
        acc = cot_ref[0, r, c0 : c0 + CHUNK, :].astype(F32)
        for i in range(3):
            for j in range(3):
                acc = acc + cw[3 * i + j : 3 * i + j + 1] * gp[r + 4 - 2 * i, pl.ds(PAD + 2 - 2 * j + c0, CHUNK), :]
        dx[0, r, c0 : c0 + CHUNK, :] = acc.astype(BF16)
        if c0 == 0:
            edge[0, r] = acc[:16]
        if c0 == COLS - CHUNK:
            edge[1, r] = acc[CHUNK - 16 :]


def kernel(
    act, cot, cw_ref, gain_ref, wi, wo, scale_ref, nb,
    dx, o_conv, o_gain, o_in, o_out, o_scale,
    xp, gp, wd, wn, sc, nm, iv, hg, ng, gb, og, ig, tg, edge,
    bands, gathered, stage, picked, corner_out, corner_in, halo, ghalo, strips, returned,
    big, small, part1, smallz, c2, part2, smalla, s2, c3, part3,
    seam_s, seam_r, ret_s, ret_r, near_s, near_r, one_s, one_r, two_s, two_r, three_s, three_r, za_s, za_r, zb_s, zb_r,
):
    f, s = lax.axis_index("face"), lax.axis_index("slab")
    x_lo, z, core = s // 16, (s // 2) % DEPTH, s % 2
    a = f * 4 + x_lo * 2 + core
    mirror = SLABS - 1 - s
    up, down = (s + SLABS - 1) % SLABS, (s + 1) % SLABS

    def in_plane(j):
        other = (a + j) % PLANE
        return other, (other // 4, ((other // 2) % 2) * 16 + z * 2 + other % 2)

    def in_depth(j):
        other = (z + j) % DEPTH
        return other, (f, x_lo * 16 + other * 2 + core)

    def loop(low, high, step):
        def body(j, carry):
            step(j)
            return carry

        lax.fori_loop(low, high, body, 0)

    barrier = pltpu.get_barrier_semaphore()

    def greet(device):
        pl.semaphore_signal(barrier, inc=1, device_id=device, device_id_type=MESH)

    greet((f, up))
    greet((f, down))
    loop(0, FACES, lambda j: greet(((f + j) % FACES, mirror)))
    loop(1, PLANE, lambda j: greet(in_plane(j)[1]))
    loop(1, DEPTH, lambda j: greet(in_depth(j)[1]))

    for r in range(ROWS):
        left = act[0, r, 0:16, :].astype(F32)
        right = act[0, r, COLS - 16 : COLS, :].astype(F32)
        for q in range(2):
            stage[0, q * 8 + r : q * 8 + r + 1, :] = left[q : q + 1]
            stage[1, q * 8 + r : q * 8 + r + 1, :] = right[15 - q : 16 - q]
    bands[...] = stage[...].astype(BF16)
    gathered[0, f] = bands[...]

    pl.semaphore_wait(barrier, 2 + FACES + PLANE - 1 + DEPTH - 1)

    def copy(src, dst, send, recv, device):
        return pltpu.make_async_remote_copy(
            src_ref=src, dst_ref=dst, send_sem=send, recv_sem=recv, device_id=device, device_id_type=MESH
        )

    def seam_copy(src, dst, sends, recvs, k, j):
        device = ((f + j) % FACES, mirror if k else s)
        return copy(src, dst.at[k, f], sends.at[k * FACES + j], recvs.at[k * FACES + f], device)

    def seam_start(src, dst, sends, recvs):
        loop(1, FACES, lambda j: seam_copy(src, dst, sends, recvs, 0, j).start())
        loop(0, FACES, lambda j: seam_copy(src, dst, sends, recvs, 1, j).start())

    def seam_wait(src, dst, sends, recvs):
        def arrived(k, j):
            face = (f + j) % FACES
            copy(src, dst.at[k, face], sends.at[k * FACES + j], recvs.at[k * FACES + face], (face, s)).wait_recv()

        loop(1, FACES, lambda j: arrived(0, j))
        loop(0, FACES, lambda j: arrived(1, j))

    def seam_sent(src, dst, sends, recvs):
        loop(1, FACES, lambda j: seam_copy(src, dst, sends, recvs, 0, j).wait_send())
        loop(0, FACES, lambda j: seam_copy(src, dst, sends, recvs, 1, j).wait_send())

    def pick(src):
        out = []
        for e in range(2):
            sf, se, k = nb[0, 0, e, 0], nb[0, 0, e, 2], nb[0, 0, e, 3]
            picked[e] = src[k, sf, se].astype(F32)
            out.append([
                [jnp.where(k == 1, picked[e, q * 8 + 7 - r : q * 8 + 8 - r, :], picked[e, q * 8 + r : q * 8 + r + 1, :]) for r in range(ROWS)]
                for q in range(2)
            ])
        return out

    halo_up = copy(act.at[0, pl.ds(0, 2)], halo.at[1], near_s.at[0], near_r.at[1], (f, up))
    halo_down = copy(act.at[0, pl.ds(ROWS - 2, 2)], halo.at[0], near_s.at[1], near_r.at[0], (f, down))
    corner_up = copy(corner_out.at[0], corner_in.at[1], near_s.at[2], near_r.at[3], (f, up))
    corner_down = copy(corner_out.at[1], corner_in.at[0], near_s.at[3], near_r.at[2], (f, down))
    grad_up = copy(gb.at[pl.ds(0, 2)], ghalo.at[1], near_s.at[4], near_r.at[5], (f, up))
    grad_down = copy(gb.at[pl.ds(ROWS - 2, 2)], ghalo.at[0], near_s.at[5], near_r.at[4], (f, down))

    seam_start(bands, gathered, seam_s, seam_r)
    halo_up.start()
    halo_down.start()

    gain, scale = gain_ref[...], scale_ref[...]
    cw = cw_ref[...]
    prepare(wi[...], wo[...], gain, scale, wd, wn)
    og[...] = jnp.zeros_like(og)
    ig[...] = jnp.zeros_like(ig)
    tg[...] = jnp.zeros_like(tg)
    for r in range(ROWS + 4):
        gp[r, 0:PAD, :] = jnp.zeros((PAD, CH), F32)
        gp[r, PAD + COLS :, :] = jnp.zeros((PAD, CH), F32)

    def own(r):
        xp[r + 2, PAD : PAD + COLS, :] = act[0, r].astype(F32)

    loop(0, ROWS, own)

    seam_wait(bands, gathered, seam_s, seam_r)
    strip = pick(gathered)
    for r in range(ROWS):
        for q in range(2):
            xp[r + 2, PAD - 1 - q : PAD - q, :] = strip[0][q][r]
            xp[r + 2, PAD + COLS + q : PAD + COLS + q + 1, :] = strip[1][q][r]
    for e in range(2):
        for q in range(2):
            for t in range(2):
                place = e * 4 + q * 2 + t
                corner_out[0, place : place + 1, :] = strip[e][q][t]
                corner_out[1, place : place + 1, :] = strip[e][q][ROWS - 2 + t]
    corner_up.start()
    corner_down.start()

    def rows_of(low, high):
        loop(low, high, lambda r: row_pass(r, cw, gain, xp, cot, wi, wd, wn, sc, nm, iv, hg, ng, gp, gb, og, ig, tg))

    rows_of(2, 6)

    halo_up.wait_recv()
    halo_down.wait_recv()
    corner_up.wait_recv()
    corner_down.wait_recv()
    inside = (jnp.where(s == 0, 0.0, 1.0), jnp.where(s == SLABS - 1, 0.0, 1.0))
    for side in range(2):
        for t in range(2):
            row = t + side * (ROWS + 2)
            xp[row, PAD : PAD + COLS, :] = halo[side, t].astype(F32) * inside[side]
            for q in range(2):
                left, right = q * 2 + t, 4 + q * 2 + t
                xp[row, PAD - 1 - q : PAD - q, :] = corner_in[side, left : left + 1, :] * inside[side]
                xp[row, PAD + COLS + q : PAD + COLS + q + 1, :] = corner_in[side, right : right + 1, :] * inside[side]

    rows_of(0, 2)
    grad_up.start()
    rows_of(ROWS - 2, ROWS)
    grad_down.start()

    products = og[...].T
    out_part = products * (0.5 * FACTOR * scale)
    in_part = ig[...] * FACTOR
    for b in range(HID // SHARE):
        big[b] = out_part[b * SHARE : (b + 1) * SHARE].astype(BF16)
    for b in range(HID // CH):
        for t in range(CH // SHARE):
            big[HID // SHARE + b * (CH // SHARE) + t] = in_part[t * SHARE : (t + 1) * SHARE, b * CH : (b + 1) * CH].astype(BF16)
    small[...] = jnp.zeros_like(small)
    small[0:9, :] = jnp.sum(tg[...], 1) * FACTOR
    in_sum = jnp.sum((in_part * wi[...].astype(F32)).T, 0, keepdims=True)
    small[9:10, :] = in_sum / gain
    small[10:11, :] = jnp.sum(products * wo[...].astype(F32), 0, keepdims=True) * (0.5 * FACTOR)

    def plane_copy(src, dst, sends, recvs, j):
        other, device = in_plane(j)
        return copy(src(other), dst.at[a], sends.at[j], recvs.at[a], device)

    def plane_wait(dst, recvs, j):
        other, device = in_plane(j)
        copy(dst.at[other], dst.at[other], recvs.at[other], recvs.at[other], device).wait_recv()

    def depth_copy(src, dst, sends, recvs, j):
        other, device = in_depth(j)
        return copy(src, dst.at[z], sends.at[j], recvs.at[z], device)

    def depth_wait(dst, recvs, j):
        other, device = in_depth(j)
        copy(dst.at[other], dst.at[other], recvs.at[other], recvs.at[other], device).wait_recv()

    one = partial(plane_copy, lambda other: big.at[other], part1, one_s, one_r)
    two = partial(depth_copy, c2, part2, za_s, za_r)
    three = partial(plane_copy, lambda other: c3, part3, three_s, three_r)
    small_one = partial(depth_copy, small, smallz, zb_s, zb_r)
    small_two = partial(plane_copy, lambda other: s2, smalla, two_s, two_r)

    loop(1, PLANE, lambda j: one(j).start())
    loop(1, DEPTH, lambda j: small_one(j).start())
    part1[a] = big[a]
    smallz[z] = small[...]

    def transposed_rows(low, high):
        loop(low, high, lambda r: transposed_row(r, cw, gp, cot, dx, edge))

    transposed_rows(2, 6)

    grad_up.wait_recv()
    grad_down.wait_recv()
    for side in range(2):
        for t in range(2):
            gp[t + side * (ROWS + 2), PAD : PAD + COLS, :] = ghalo[side, t].astype(F32) * inside[side]
    for r in range(ROWS):
        left, right = jnp.zeros((8, CH), F32), jnp.zeros((8, CH), F32)
        for i in range(3):
            left = left + cw[3 * i : 3 * i + 1] * gp[r + 4 - 2 * i, PAD : PAD + 8, :]
            right = right + cw[3 * i + 2 : 3 * i + 3] * gp[r + 4 - 2 * i, PAD + COLS - 8 : PAD + COLS, :]
        for q in range(2):
            stage[0, q * 8 + r : q * 8 + r + 1, :] = left[1 - q : 2 - q]
            stage[1, q * 8 + r : q * 8 + r + 1, :] = right[6 + q : 7 + q]
    strips[...] = stage[...].astype(BF16)
    returned[0, f] = strips[...]
    seam_start(strips, returned, ret_s, ret_r)

    transposed_rows(0, 2)
    transposed_rows(ROWS - 2, ROWS)

    loop(1, PLANE, lambda j: plane_wait(part1, one_r, j))
    loop(1, DEPTH, lambda j: depth_wait(smallz, zb_r, j))
    total = part1[0].astype(F32)
    for b in range(1, PLANE):
        total = total + part1[b].astype(F32)
    c2[...] = total.astype(BF16)
    s2[...] = jnp.sum(smallz[...], 0)
    part2[z] = c2[...]
    smalla[a] = s2[...]
    loop(1, DEPTH, lambda j: two(j).start())
    loop(1, PLANE, lambda j: small_two(j).start())

    seam_wait(strips, returned, ret_s, ret_r)
    back = pick(returned)
    for r in range(ROWS):
        for q in range(2):
            edge[0, r, q : q + 1, :] += back[0][q][r]
            edge[1, r, 15 - q : 16 - q, :] += back[1][q][r]
        dx[0, r, 0:16, :] = edge[0, r].astype(BF16)
        dx[0, r, COLS - 16 : COLS, :] = edge[1, r].astype(BF16)

    loop(1, DEPTH, lambda j: depth_wait(part2, za_r, j))
    c3[...] = jnp.sum(part2[...].astype(F32), 0).astype(BF16)
    part3[a] = c3[...]
    loop(1, PLANE, lambda j: three(j).start())

    loop(1, PLANE, lambda j: plane_wait(smalla, two_r, j))
    sums = smalla[0]
    for b in range(1, PLANE):
        sums = sums + smalla[b]
    o_conv[...] = sums[0:9]
    o_gain[...] = sums[9:10]
    o_scale[...] = sums[10:11]

    seam_sent(bands, gathered, seam_s, seam_r)
    seam_sent(strips, returned, ret_s, ret_r)
    for sent in (halo_up, halo_down, corner_up, corner_down, grad_up, grad_down):
        sent.wait_send()
    loop(1, PLANE, lambda j: one(j).wait_send())
    loop(1, PLANE, lambda j: small_two(j).wait_send())
    loop(1, DEPTH, lambda j: two(j).wait_send())
    loop(1, DEPTH, lambda j: small_one(j).wait_send())

    loop(1, PLANE, lambda j: plane_wait(part3, three_r, j))
    for b in range(HID // SHARE):
        o_out[b * SHARE : (b + 1) * SHARE, :] = part3[b].astype(F32)
    for b in range(HID // CH):
        for t in range(CH // SHARE):
            o_in[t * SHARE : (t + 1) * SHARE, b * CH : (b + 1) * CH] = part3[HID // SHARE + b * (CH // SHARE) + t].astype(F32)
    loop(1, PLANE, lambda j: three(j).wait_send())


def body(activations, cotangent, conv_weight, norm_gain, w_in, w_out, layer_scale, neighbours):
    vmem = pl.BlockSpec(memory_space=pltpu.VMEM)
    smem = pl.BlockSpec(memory_space=pltpu.SMEM)
    dma = pltpu.SemaphoreType.DMA

    def buf(*shape, dtype=F32):
        return pltpu.VMEM(shape, dtype)

    half = partial(buf, dtype=BF16)
    outs = pl.pallas_call(
        kernel,
        out_shape=[
            jax.ShapeDtypeStruct((1, ROWS, COLS, CH), BF16),
            jax.ShapeDtypeStruct((9, CH), F32),
            jax.ShapeDtypeStruct((1, CH), F32),
            jax.ShapeDtypeStruct((CH, HID), F32),
            jax.ShapeDtypeStruct((HID, CH), F32),
            jax.ShapeDtypeStruct((1, CH), F32),
        ],
        in_specs=[vmem] * 7 + [smem],
        out_specs=[vmem] * 6,
        scratch_shapes=[
            buf(ROWS + 4, WIDE, CH), buf(ROWS + 4, WIDE, CH), half(CH, HID), half(HID, 2 * CH),
            half(COLS, CH), buf(COLS, CH), buf(COLS, CH), half(COLS, HID), buf(COLS, 2 * CH), half(ROWS, COLS, CH),
            buf(CH, HID), buf(CH, HID), buf(9, 8, CH), buf(2, ROWS, 16, CH),
            half(2, 16, CH), half(2, FACES, 2, 16, CH), buf(2, 16, CH), buf(2, 16, CH), buf(2, 8, CH), buf(2, 8, CH),
            half(2, 2, COLS, CH), half(2, 2, COLS, CH), half(2, 16, CH), half(2, FACES, 2, 16, CH),
            half(PLANE, SHARE, CH), buf(16, CH), half(PLANE, SHARE, CH), buf(DEPTH, 16, CH), half(SHARE, CH),
            half(DEPTH, SHARE, CH), buf(PLANE, 16, CH), buf(16, CH), half(SHARE, CH), half(PLANE, SHARE, CH),
            dma((16,)), dma((16,)), dma((16,)), dma((16,)), dma((6,)), dma((6,)),
            dma((PLANE,)), dma((PLANE,)), dma((PLANE,)), dma((PLANE,)), dma((PLANE,)), dma((PLANE,)),
            dma((DEPTH,)), dma((DEPTH,)), dma((DEPTH,)), dma((DEPTH,)),
        ],
        compiler_params=pltpu.CompilerParams(collective_id=0, has_side_effects=True, vmem_limit_bytes=56 * 2**20),
    )(
        activations, cotangent, conv_weight, norm_gain.reshape(1, CH), w_in, w_out, layer_scale.reshape(1, CH), neighbours
    )
    dx, conv_grad, gain_grad, in_grad, out_grad, scale_grad = outs
    return dx, conv_grad, gain_grad.reshape(CH), in_grad, out_grad, scale_grad.reshape(CH)


def solution(mesh):
    cells = P("face", "slab", None, None)
    return jax.shard_map(
        body,
        mesh=mesh,
        in_specs=(cells, cells, P(), P(), P(), P(), P(), cells),
        out_specs=(cells, P(), P(), P(), P(), P()),
        check_vma=False,
    )
```

```python
import math
from functools import partial

import jax
import jax.numpy as jnp
from jax import lax
from jax.experimental import pallas as pl
from jax.experimental.pallas import tpu as pltpu
from jax.sharding import PartitionSpec as P

F32, BF16 = jnp.float32, jnp.bfloat16
FACES, SLABS = 8, 32
DEPTH = 8
PLANE = 32
ROWS, COLS, CH, HID = 8, 512, 128, 512
PAD = 8
WIDE = COLS + 2 * PAD
CHUNK = 64
SHARE = 32
CELLS = FACES * SLABS * ROWS * COLS
FACTOR = float(CELLS) ** (-0.5)
EPSILON = 1e-6
SQRT_HALF = math.sqrt(0.5)
EXPONENT = -math.log2(math.e)
BIAS = math.log2(2 / math.sqrt(2 * math.pi))
MESH = pl.DeviceIdType.MESH


def dot(a, b, dims=((1,), (0,))):
    return lax.dot_general(a, b, (dims, ((), ())), preferred_element_type=F32)


def prepare(wi, wo, scale, wd_ref, wn_ref):
    wd_ref[...] = (wo.astype(F32) * (0.5 * scale)).T.astype(BF16)
    wn_ref[...] = wi.astype(F32).T.astype(BF16)


def forward(pieces, size, cw, gain, xp, cv, wi_ref, wd_ref, sc, nm, iv, hg, og, ig):
    total = len(pieces) * size
    for n, (r, c0) in enumerate(pieces):
        acc = None
        for i in range(3):
            for j in range(3):
                t = cw[3 * i + j : 3 * i + j + 1] * xp[r + 2 * i, pl.ds(PAD - 2 + 2 * j + c0, size), :]
                acc = t if acc is None else acc + t
        centred = acc - jnp.mean(acc, -1, keepdims=True)
        variance = jnp.mean(centred * centred, -1, keepdims=True)
        inverse = jnp.broadcast_to(lax.rsqrt(variance + EPSILON), (size, CH))
        normed = centred * inverse
        sc[n * size : (n + 1) * size, :] = (normed * gain).astype(BF16)
        nm[r, c0 : c0 + size, :] = normed
        iv[r, c0 : c0 + size, :] = inverse
    cot = jnp.concatenate([cv[r, c0 : c0 + size, :] for r, c0 in pieces], 0)
    scaled = sc[:total, :]
    hidden = dot(scaled, wi_ref[...])
    upstream = dot(cot, wd_ref[...])
    x = hidden * SQRT_HALF
    twice = 1.0 + lax.erf(x)
    activated = (hidden * twice).astype(BF16)
    density = jnp.exp2(x * x * EXPONENT + BIAS)
    hidden_grad = ((twice + hidden * density) * upstream).astype(BF16)
    for n, (r, c0) in enumerate(pieces):
        hg[r, c0 : c0 + size, :] = hidden_grad[n * size : (n + 1) * size]
    og[...] += dot(cot, activated, ((0,), (0,)))
    ig[...] += dot(scaled, hidden_grad, ((0,), (0,)))


def backward(r, gain, xp, wn_ref, nm, iv, hg, ng, gp, gb, tg):
    ng[...] = dot(hg[r], wn_ref[...])
    for c0 in range(0, COLS, CHUNK):
        d = ng[c0 : c0 + CHUNK, :] * gain
        normed = nm[r, c0 : c0 + CHUNK, :]
        d_mean = jnp.mean(d, -1, keepdims=True)
        dn_mean = jnp.mean(d * normed, -1, keepdims=True)
        gb16 = (iv[r, c0 : c0 + CHUNK, :] * (d - d_mean - normed * dn_mean)).astype(BF16)
        gb[r, c0 : c0 + CHUNK, :] = gb16
        g = gb16.astype(F32)
        gp[r + 2, PAD + c0 : PAD + c0 + CHUNK, :] = g
        for i in range(3):
            for j in range(3):
                t = g * xp[r + 2 * i, pl.ds(PAD - 2 + 2 * j + c0, CHUNK), :]
                tg[3 * i + j] += t.reshape(CHUNK // 8, 8, CH).sum(0)


def transposed_row(r, cw, gp, cv, dxv, edge):
    for c0 in range(0, COLS, CHUNK):
        acc = cv[r, c0 : c0 + CHUNK, :].astype(F32)
        for i in range(3):
            for j in range(3):
                acc = acc + cw[3 * i + j : 3 * i + j + 1] * gp[r + 4 - 2 * i, pl.ds(PAD + 2 - 2 * j + c0, CHUNK), :]
        dxv[r, c0 : c0 + CHUNK, :] = acc.astype(BF16)
        if c0 == 0:
            edge[0, r] = acc[:16]
        if c0 == COLS - CHUNK:
            edge[1, r] = acc[CHUNK - 16 :]


def kernel(
    act, cot, cw_hbm, gain_hbm, wi_hbm, wo_hbm, scale_hbm, nb_hbm,
    dx, part3,
    cw_ref, gain_ref, scale_ref, nb, av, cv, wi, wo, dxv, xp, gp, wd, wn, sc, nm, iv, hg, ng, gb, og, ig, tg, edge,
    bands, gathered, stage, picked, corner_out, corner_in, halo, ghalo, strips, returned,
    big, small, part1, c2, part2, c3,
    act_s, cot_s, wgt_s, dx_s, own_s,
    seam_s, seam_r, ret_s, ret_r, near_s, near_r, one_s, one_r, three_s, three_r, za_s, za_r,
):
    f, s = lax.axis_index("face"), lax.axis_index("slab")
    x_lo, z, core = s // 16, (s // 2) % DEPTH, s % 2
    a = f * 4 + x_lo * 2 + core
    mirror = SLABS - 1 - s
    up, down = (s + SLABS - 1) % SLABS, (s + 1) % SLABS

    def in_plane(j):
        other = (a + j) % PLANE
        return other, (other // 4, ((other // 2) % 2) * 16 + z * 2 + other % 2)

    def in_depth(j):
        other = (z + j) % DEPTH
        return other, (f, x_lo * 16 + other * 2 + core)

    def loop(low, high, step):
        def body(j, carry):
            step(j)
            return carry

        lax.fori_loop(low, high, body, 0)

    act_in = [pltpu.make_async_copy(act.at[0, r], av.at[r], act_s.at[r]) for r in range(ROWS)]
    cot_in = [pltpu.make_async_copy(cot.at[0, r], cv.at[r], cot_s.at[r]) for r in range(ROWS)]
    wi_in = pltpu.make_async_copy(wi_hbm, wi, wgt_s.at[0])
    wo_in = pltpu.make_async_copy(wo_hbm, wo, wgt_s.at[1])
    little = [(nb_hbm, nb), (cw_hbm, cw_ref), (gain_hbm, gain_ref), (scale_hbm, scale_ref)]
    little_in = [pltpu.make_async_copy(src, dst, wgt_s.at[2 + n]) for n, (src, dst) in enumerate(little)]
    for c in act_in + little_in + [wi_in, wo_in] + cot_in:
        c.start()

    barrier = pltpu.get_barrier_semaphore()

    def greet(device):
        pl.semaphore_signal(barrier, inc=1, device_id=device, device_id_type=MESH)

    loop(0, FACES, lambda j: greet(((f + j) % FACES, mirror)))
    greet((f, up))
    greet((f, down))
    loop(1, PLANE, lambda j: greet(in_plane(j)[1]))
    loop(1, DEPTH, lambda j: greet(in_depth(j)[1]))

    og[...] = jnp.zeros_like(og)
    ig[...] = jnp.zeros_like(ig)
    tg[...] = jnp.zeros_like(tg)
    for r in range(ROWS + 4):
        gp[r, 0:PAD, :] = jnp.zeros((PAD, CH), F32)
        gp[r, PAD + COLS :, :] = jnp.zeros((PAD, CH), F32)
    for c in act_in:
        c.wait()
    for r in range(ROWS):
        left = av[r, 0:16, :].astype(F32)
        right = av[r, COLS - 16 : COLS, :].astype(F32)
        for q in range(2):
            stage[0, q * 8 + r : q * 8 + r + 1, :] = left[q : q + 1]
            stage[1, q * 8 + r : q * 8 + r + 1, :] = right[15 - q : 16 - q]
    bands[...] = stage[...].astype(BF16)
    gathered[0, f] = bands[...]

    def own(r):
        xp[r + 2, PAD : PAD + COLS, :] = av[r].astype(F32)

    loop(0, ROWS, own)

    pl.semaphore_wait(barrier, 2 + FACES + PLANE - 1 + DEPTH - 1)

    def copy(src, dst, send, recv, device):
        return pltpu.make_async_remote_copy(
            src_ref=src, dst_ref=dst, send_sem=send, recv_sem=recv, device_id=device, device_id_type=MESH
        )

    def seam_copy(src, dst, sends, recvs, k, j):
        device = ((f + j) % FACES, mirror if k else s)
        return copy(src, dst.at[k, f], sends.at[k * FACES + j], recvs.at[k * FACES + f], device)

    def seam_start(src, dst, sends, recvs):
        loop(1, FACES, lambda j: seam_copy(src, dst, sends, recvs, 0, j).start())
        loop(0, FACES, lambda j: seam_copy(src, dst, sends, recvs, 1, j).start())

    def seam_wait(src, dst, sends, recvs):
        def arrived(k, j):
            face = (f + j) % FACES
            copy(src, dst.at[k, face], sends.at[k * FACES + j], recvs.at[k * FACES + face], (face, s)).wait_recv()

        loop(1, FACES, lambda j: arrived(0, j))
        loop(0, FACES, lambda j: arrived(1, j))

    def seam_sent(src, dst, sends, recvs):
        loop(1, FACES, lambda j: seam_copy(src, dst, sends, recvs, 0, j).wait_send())
        loop(0, FACES, lambda j: seam_copy(src, dst, sends, recvs, 1, j).wait_send())

    def pick(src):
        out = []
        for e in range(2):
            sf, se, k = nb[0, 0, e, 0], nb[0, 0, e, 2], nb[0, 0, e, 3]
            picked[e] = src[k, sf, se].astype(F32)
            out.append([
                [jnp.where(k == 1, picked[e, q * 8 + 7 - r : q * 8 + 8 - r, :], picked[e, q * 8 + r : q * 8 + r + 1, :]) for r in range(ROWS)]
                for q in range(2)
            ])
        return out

    halo_up = copy(av.at[pl.ds(0, 2)], halo.at[1], near_s.at[0], near_r.at[1], (f, up))
    halo_down = copy(av.at[pl.ds(ROWS - 2, 2)], halo.at[0], near_s.at[1], near_r.at[0], (f, down))
    corner_up = copy(corner_out.at[0], corner_in.at[1], near_s.at[2], near_r.at[3], (f, up))
    corner_down = copy(corner_out.at[1], corner_in.at[0], near_s.at[3], near_r.at[2], (f, down))
    grad_up = copy(gb.at[pl.ds(0, 2)], ghalo.at[1], near_s.at[4], near_r.at[5], (f, up))
    grad_down = copy(gb.at[pl.ds(ROWS - 2, 2)], ghalo.at[0], near_s.at[5], near_r.at[4], (f, down))

    halo_up.start()
    halo_down.start()
    seam_start(bands, gathered, seam_s, seam_r)

    for c in little_in:
        c.wait()
    gain, scale = gain_ref[...], scale_ref[...]
    cw = cw_ref[...]
    wi_in.wait()
    wo_in.wait()
    prepare(wi[...], wo[...], scale, wd, wn)
    for c in cot_in:
        c.wait()

    def cells(pieces, size):
        forward(pieces, size, cw, gain, xp, cv, wi, wd, sc, nm, iv, hg, og, ig)

    def middle(r):
        cells([(r, c0) for c0 in range(64, COLS - 64, 64)], 64)

    def sides(rows):
        cells([(r, c0) for r in rows for c0 in (0, COLS - 64)], 64)

    loop(2, ROWS - 2, middle)

    seam_wait(bands, gathered, seam_s, seam_r)
    strip = pick(gathered)
    for r in range(ROWS):
        for q in range(2):
            xp[r + 2, PAD - 1 - q : PAD - q, :] = strip[0][q][r]
            xp[r + 2, PAD + COLS + q : PAD + COLS + q + 1, :] = strip[1][q][r]
    for e in range(2):
        for q in range(2):
            for t in range(2):
                place = e * 4 + q * 2 + t
                corner_out[0, place : place + 1, :] = strip[e][q][t]
                corner_out[1, place : place + 1, :] = strip[e][q][ROWS - 2 + t]
    corner_up.start()
    corner_down.start()

    sides((2, 3, 4, 5))

    halo_up.wait_recv()
    halo_down.wait_recv()
    inside = (jnp.where(s == 0, 0.0, 1.0), jnp.where(s == SLABS - 1, 0.0, 1.0))
    for side in range(2):
        for t in range(2):
            row = t + side * (ROWS + 2)
            xp[row, PAD : PAD + COLS, :] = halo[side, t].astype(F32) * inside[side]
    loop(0, 4, lambda n: middle(n + n // 2 * 4))

    corner_up.wait_recv()
    corner_down.wait_recv()
    for side in range(2):
        for t in range(2):
            row = t + side * (ROWS + 2)
            for q in range(2):
                left, right = q * 2 + t, 4 + q * 2 + t
                xp[row, PAD - 1 - q : PAD - q, :] = corner_in[side, left : left + 1, :] * inside[side]
                xp[row, PAD + COLS + q : PAD + COLS + q + 1, :] = corner_in[side, right : right + 1, :] * inside[side]

    sides((0, 1, 6, 7))

    products = og[...].T
    out_part = products * (0.5 * FACTOR * scale)
    in_part = ig[...] * FACTOR
    for b in range(HID // SHARE):
        big[b] = out_part[b * SHARE : (b + 1) * SHARE].astype(BF16)
    for b in range(HID // CH):
        for t in range(CH // SHARE):
            big[HID // SHARE + b * (CH // SHARE) + t] = in_part[t * SHARE : (t + 1) * SHARE, b * CH : (b + 1) * CH].astype(BF16)

    def plane_copy(src, dst, sends, recvs, j):
        other, device = in_plane(j)
        return copy(src(other), dst.at[a], sends.at[j], recvs.at[a], device)

    def plane_wait(dst, recvs, j):
        other, device = in_plane(j)
        copy(dst.at[other], dst.at[other], recvs.at[other], recvs.at[other], device).wait_recv()

    def depth_copy(src, dst, sends, recvs, j):
        other, device = in_depth(j)
        return copy(src, dst.at[z], sends.at[j], recvs.at[z], device)

    def depth_wait(dst, recvs, j):
        other, device = in_depth(j)
        copy(dst.at[other], dst.at[other], recvs.at[other], recvs.at[other], device).wait_recv()

    one = partial(plane_copy, lambda other: big.at[other], part1, one_s, one_r)
    two = partial(depth_copy, c2, part2, za_s, za_r)
    three = partial(plane_copy, lambda other: c3, part3, three_s, three_r)

    loop(1, PLANE, lambda j: one(j).start())
    part1[a] = big[a]

    def rows_back(low, high):
        loop(low, high, lambda r: backward(r, gain, xp, wn, nm, iv, hg, ng, gp, gb, tg))

    rows_back(0, 2)
    grad_up.start()
    rows_back(ROWS - 2, ROWS)
    grad_down.start()
    rows_back(2, ROWS - 2)

    small[...] = jnp.zeros_like(small)
    small[0:9, :] = jnp.sum(tg[...], 1) * FACTOR
    in_sum = jnp.sum((ig[...] * wi[...].astype(F32)).T, 0, keepdims=True)
    small[9:10, :] = in_sum / gain * FACTOR
    small[10:11, :] = jnp.sum(og[...].T * wo[...].astype(F32), 0, keepdims=True) * (0.5 * FACTOR)

    loop(1, PLANE, lambda j: plane_wait(part1, one_r, j))
    total = part1[0].astype(F32)
    for b in range(1, PLANE):
        total = total + part1[b].astype(F32)
    c2[:SHARE, :] = total.astype(BF16)
    c2[SHARE:, :] = small[...].astype(BF16)
    part2[z] = c2[...]
    loop(1, DEPTH, lambda j: two(j).start())

    grad_up.wait_recv()
    grad_down.wait_recv()
    for side in range(2):
        for t in range(2):
            gp[t + side * (ROWS + 2), PAD : PAD + COLS, :] = ghalo[side, t].astype(F32) * inside[side]
    for r in range(ROWS):
        left, right = jnp.zeros((8, CH), F32), jnp.zeros((8, CH), F32)
        for i in range(3):
            left = left + cw[3 * i : 3 * i + 1] * gp[r + 4 - 2 * i, PAD : PAD + 8, :]
            right = right + cw[3 * i + 2 : 3 * i + 3] * gp[r + 4 - 2 * i, PAD + COLS - 8 : PAD + COLS, :]
        for q in range(2):
            stage[0, q * 8 + r : q * 8 + r + 1, :] = left[1 - q : 2 - q]
            stage[1, q * 8 + r : q * 8 + r + 1, :] = right[6 + q : 7 + q]
    strips[...] = stage[...].astype(BF16)
    returned[0, f] = strips[...]
    seam_start(strips, returned, ret_s, ret_r)

    def transposed_rows(low, high):
        loop(low, high, lambda r: transposed_row(r, cw, gp, cv, dxv, edge))

    transposed_rows(0, ROWS)

    loop(1, DEPTH, lambda j: depth_wait(part2, za_r, j))
    c3[...] = jnp.sum(part2[...].astype(F32), 0).astype(BF16)
    loop(1, PLANE, lambda j: three(j).start())
    own_share = pltpu.make_async_copy(c3, part3.at[a], own_s.at[0])
    own_share.start()

    seam_wait(strips, returned, ret_s, ret_r)
    back = pick(returned)
    for r in range(ROWS):
        for q in range(2):
            edge[0, r, q : q + 1, :] += back[0][q][r]
            edge[1, r, 15 - q : 16 - q, :] += back[1][q][r]
        dxv[r, 0:16, :] = edge[0, r].astype(BF16)
        dxv[r, COLS - 16 : COLS, :] = edge[1, r].astype(BF16)
    dx_out = [pltpu.make_async_copy(dxv.at[r], dx.at[0, r], dx_s.at[r]) for r in range(ROWS)]
    for c in dx_out:
        c.start()

    seam_sent(bands, gathered, seam_s, seam_r)
    seam_sent(strips, returned, ret_s, ret_r)
    for sent in (halo_up, halo_down, corner_up, corner_down, grad_up, grad_down):
        sent.wait_send()
    loop(1, PLANE, lambda j: one(j).wait_send())
    loop(1, DEPTH, lambda j: two(j).wait_send())
    for c in dx_out:
        c.wait()
    own_share.wait()
    loop(1, PLANE, lambda j: three(j).wait_send())
    loop(1, PLANE, lambda j: plane_wait(part3, three_r, j))


def finish(dx_in, parts, dx, o_conv, o_gain, o_in, o_out, o_scale, sem):
    moved = [pltpu.make_async_copy(dx_in.at[0, r], dx.at[0, r], sem.at[r]) for r in range(ROWS)]
    for c in moved:
        c.start()
    for b in range(HID // SHARE):
        o_out[b * SHARE : (b + 1) * SHARE, :] = parts[b, :SHARE, :].astype(F32)
    for b in range(HID // CH):
        for t in range(CH // SHARE):
            o_in[t * SHARE : (t + 1) * SHARE, b * CH : (b + 1) * CH] = parts[HID // SHARE + b * (CH // SHARE) + t, :SHARE, :].astype(F32)
    sums = parts[0, SHARE:, :].astype(F32)
    for b in range(1, PLANE):
        sums = sums + parts[b, SHARE:, :].astype(F32)
    o_conv[...] = sums[0:9]
    o_gain[...] = sums[9:10]
    o_scale[...] = sums[10:11]
    for c in moved:
        c.wait()


def body(activations, cotangent, conv_weight, norm_gain, w_in, w_out, layer_scale, neighbours):
    vmem = pl.BlockSpec(memory_space=pltpu.VMEM)
    anywhere = pl.BlockSpec(memory_space=pl.ANY)
    dma = pltpu.SemaphoreType.DMA

    def buf(*shape, dtype=F32):
        return pltpu.VMEM(shape, dtype)

    half = partial(buf, dtype=BF16)
    cells = jax.ShapeDtypeStruct((1, ROWS, COLS, CH), BF16)
    dx, parts = pl.pallas_call(
        kernel,
        out_shape=[half(1, ROWS, COLS, CH), half(PLANE, SHARE + 16, CH)],
        in_specs=[anywhere] * 8,
        out_specs=[anywhere, anywhere],
        scratch_shapes=[
            buf(9, CH), buf(1, CH), buf(1, CH), pltpu.SMEM((1, 1, 2, 4), jnp.int32),
            half(ROWS, COLS, CH), half(ROWS, COLS, CH), half(CH, HID), half(HID, CH), half(ROWS, COLS, CH),
            buf(ROWS + 4, WIDE, CH), buf(ROWS + 4, WIDE, CH), half(CH, HID), half(HID, CH),
            half(COLS, CH), buf(ROWS, COLS, CH), buf(ROWS, COLS, CH), half(ROWS, COLS, HID), buf(COLS, CH), half(ROWS, COLS, CH),
            buf(CH, HID), buf(CH, HID), buf(9, 8, CH), buf(2, ROWS, 16, CH),
            half(2, 16, CH), half(2, FACES, 2, 16, CH), buf(2, 16, CH), buf(2, 16, CH), buf(2, 8, CH), buf(2, 8, CH),
            half(2, 2, COLS, CH), half(2, 2, COLS, CH), half(2, 16, CH), half(2, FACES, 2, 16, CH),
            half(PLANE, SHARE, CH), buf(16, CH), half(PLANE, SHARE, CH), half(SHARE + 16, CH),
            half(DEPTH, SHARE + 16, CH), half(SHARE + 16, CH),
            dma((ROWS,)), dma((ROWS,)), dma((6,)), dma((ROWS,)), dma((1,)),
            dma((16,)), dma((16,)), dma((16,)), dma((16,)), dma((6,)), dma((6,)),
            dma((PLANE,)), dma((PLANE,)), dma((PLANE,)), dma((PLANE,)), dma((DEPTH,)), dma((DEPTH,)),
        ],
        compiler_params=pltpu.CompilerParams(collective_id=0, has_side_effects=True, vmem_limit_bytes=48 * 2**20),
    )(*[
        pltpu.with_memory_space_constraint(x, pltpu.HBM)
        for x in (activations, cotangent, conv_weight, norm_gain.reshape(1, CH), w_in, w_out, layer_scale.reshape(1, CH), neighbours)
    ])
    input_gradient, conv_grad, gain_grad, in_grad, out_grad, scale_grad = pl.pallas_call(
        finish,
        out_shape=[
            cells,
            jax.ShapeDtypeStruct((9, CH), F32),
            jax.ShapeDtypeStruct((1, CH), F32),
            jax.ShapeDtypeStruct((CH, HID), F32),
            jax.ShapeDtypeStruct((HID, CH), F32),
            jax.ShapeDtypeStruct((1, CH), F32),
        ],
        in_specs=[anywhere, vmem],
        out_specs=[anywhere] + [vmem] * 5,
        scratch_shapes=[dma((ROWS,))],
        compiler_params=pltpu.CompilerParams(vmem_limit_bytes=8 * 2**20),
    )(dx, parts)
    return input_gradient, conv_grad, gain_grad.reshape(CH), in_grad, out_grad, scale_grad.reshape(CH)


def solution(mesh):
    cells = P("face", "slab", None, None)
    return jax.shard_map(
        body,
        mesh=mesh,
        in_specs=(cells, cells, P(), P(), P(), P(), P(), cells),
        out_specs=(cells, P(), P(), P(), P(), P()),
        check_vma=False,
    )
```

```python
import math
from functools import partial

import jax
import jax.numpy as jnp
from jax import lax
from jax.experimental import pallas as pl
from jax.experimental.pallas import tpu as pltpu
from jax.sharding import PartitionSpec as P

F32, BF16 = jnp.float32, jnp.bfloat16
FACES, SLABS = 8, 32
DEPTH = 8
PLANE = 32
ROWS, COLS, CH, HID = 8, 512, 128, 512
PAD = 8
WIDE = COLS + 2 * PAD
CHUNK = 64
SHARE = 32
CELLS = FACES * SLABS * ROWS * COLS
FACTOR = float(CELLS) ** (-0.5)
EPSILON = 1e-6
SQRT_HALF = math.sqrt(0.5)
EXPONENT = -math.log2(math.e)
BIAS = math.log2(2 / math.sqrt(2 * math.pi))
MESH = pl.DeviceIdType.MESH


def dot(a, b, dims=((1,), (0,))):
    return lax.dot_general(a, b, (dims, ((), ())), preferred_element_type=F32)


def prepare(wi, wo, scale, wd_ref, wn_ref):
    wd_ref[...] = (wo.astype(F32) * (0.5 * scale)).T.astype(BF16)
    wn_ref[...] = wi.astype(F32).T.astype(BF16)


def forward(pieces, size, cw, gain, xp, cv, wi_ref, wd_ref, sc, nm, iv, hg, og, ig):
    total = len(pieces) * size
    for n, (r, c0) in enumerate(pieces):
        acc = None
        for i in range(3):
            for j in range(3):
                t = cw[3 * i + j : 3 * i + j + 1] * xp[r + 2 * i, pl.ds(PAD - 2 + 2 * j + c0, size), :]
                acc = t if acc is None else acc + t
        centred = acc - jnp.mean(acc, -1, keepdims=True)
        variance = jnp.mean(centred * centred, -1, keepdims=True)
        inverse = jnp.broadcast_to(lax.rsqrt(variance + EPSILON), (size, CH))
        normed = centred * inverse
        sc[n * size : (n + 1) * size, :] = (normed * gain).astype(BF16)
        nm[r, c0 : c0 + size, :] = normed
        iv[r, c0 : c0 + size, :] = inverse
    cot = jnp.concatenate([cv[r, c0 : c0 + size, :] for r, c0 in pieces], 0)
    scaled = sc[:total, :]
    hidden = dot(scaled, wi_ref[...])
    upstream = dot(cot, wd_ref[...])
    x = hidden * SQRT_HALF
    twice = 1.0 + lax.erf(x)
    activated = (hidden * twice).astype(BF16)
    density = jnp.exp2(x * x * EXPONENT + BIAS)
    hidden_grad = ((twice + hidden * density) * upstream).astype(BF16)
    for n, (r, c0) in enumerate(pieces):
        hg[r, c0 : c0 + size, :] = hidden_grad[n * size : (n + 1) * size]
    og[...] += dot(cot, activated, ((0,), (0,)))
    ig[...] += dot(scaled, hidden_grad, ((0,), (0,)))


def backward(r, gain, xp, wn_ref, nm, iv, hg, ng, gp, gb, tg):
    ng[...] = dot(hg[r], wn_ref[...])
    for c0 in range(0, COLS, CHUNK):
        d = ng[c0 : c0 + CHUNK, :] * gain
        normed = nm[r, c0 : c0 + CHUNK, :]
        d_mean = jnp.mean(d, -1, keepdims=True)
        dn_mean = jnp.mean(d * normed, -1, keepdims=True)
        gb16 = (iv[r, c0 : c0 + CHUNK, :] * (d - d_mean - normed * dn_mean)).astype(BF16)
        gb[r, c0 : c0 + CHUNK, :] = gb16
        g = gb16.astype(F32)
        gp[r + 2, PAD + c0 : PAD + c0 + CHUNK, :] = g
        for i in range(3):
            for j in range(3):
                t = g * xp[r + 2 * i, pl.ds(PAD - 2 + 2 * j + c0, CHUNK), :]
                tg[3 * i + j] += t.reshape(CHUNK // 8, 8, CH).sum(0)


def transposed_row(r, cw, gp, cv, dxv, edge):
    for c0 in range(0, COLS, CHUNK):
        acc = cv[r, c0 : c0 + CHUNK, :].astype(F32)
        for i in range(3):
            for j in range(3):
                acc = acc + cw[3 * i + j : 3 * i + j + 1] * gp[r + 4 - 2 * i, pl.ds(PAD + 2 - 2 * j + c0, CHUNK), :]
        dxv[r, c0 : c0 + CHUNK, :] = acc.astype(BF16)
        if c0 == 0:
            edge[0, r] = acc[:16]
        if c0 == COLS - CHUNK:
            edge[1, r] = acc[CHUNK - 16 :]


def kernel(
    act, cot, cw_hbm, gain_hbm, wi_hbm, wo_hbm, scale_hbm, nb_hbm,
    dx, part3, part5,
    cw_ref, gain_ref, scale_ref, nb, av, cv, wi, wo, dxv, xp, gp, wd, wn, sc, nm, iv, hg, ng, gb, og, ig, tg, edge,
    bands, gathered, stage, picked, corner_out, corner_in, gcorner_out, gcorner_in, halo, ghalo, strips, returned,
    big, small, small16, smallz, part1, c2, part2, c3, four, part4, five,
    act_s, cot_s, wgt_s, dx_s, own_s,
    seam_s, seam_r, ret_s, ret_r, near_s, near_r, one_s, one_r, three_s, three_r, za_s, za_r, zb_s, zb_r, four_s, four_r, five_s, five_r,
):
    f, s = lax.axis_index("face"), lax.axis_index("slab")
    x_lo, z, core = s // 16, (s // 2) % DEPTH, s % 2
    a = f * 4 + x_lo * 2 + core
    mirror = SLABS - 1 - s
    up, down = (s + SLABS - 1) % SLABS, (s + 1) % SLABS

    def in_plane(j):
        other = (a + j) % PLANE
        return other, (other // 4, ((other // 2) % 2) * 16 + z * 2 + other % 2)

    def in_depth(j):
        other = (z + j) % DEPTH
        return other, (f, x_lo * 16 + other * 2 + core)

    def loop(low, high, step):
        def body(j, carry):
            step(j)
            return carry

        lax.fori_loop(low, high, body, 0)

    act_in = [pltpu.make_async_copy(act.at[0, r], av.at[r], act_s.at[r]) for r in range(ROWS)]
    cot_in = [pltpu.make_async_copy(cot.at[0, r], cv.at[r], cot_s.at[r]) for r in range(ROWS)]
    wi_in = pltpu.make_async_copy(wi_hbm, wi, wgt_s.at[0])
    wo_in = pltpu.make_async_copy(wo_hbm, wo, wgt_s.at[1])
    little = [(nb_hbm, nb), (cw_hbm, cw_ref), (gain_hbm, gain_ref), (scale_hbm, scale_ref)]
    little_in = [pltpu.make_async_copy(src, dst, wgt_s.at[2 + n]) for n, (src, dst) in enumerate(little)]
    for c in act_in + little_in + [wi_in, wo_in] + cot_in:
        c.start()

    barrier = pltpu.get_barrier_semaphore()

    def greet(device):
        pl.semaphore_signal(barrier, inc=1, device_id=device, device_id_type=MESH)

    loop(0, FACES, lambda j: greet(((f + j) % FACES, mirror)))
    greet((f, up))
    greet((f, down))
    loop(1, PLANE, lambda j: greet(in_plane(j)[1]))
    loop(1, DEPTH, lambda j: greet(in_depth(j)[1]))

    og[...] = jnp.zeros_like(og)
    ig[...] = jnp.zeros_like(ig)
    tg[...] = jnp.zeros_like(tg)
    for r in range(ROWS + 4):
        gp[r, 0:PAD, :] = jnp.zeros((PAD, CH), F32)
        gp[r, PAD + COLS :, :] = jnp.zeros((PAD, CH), F32)
    for c in act_in:
        c.wait()
    for r in range(ROWS):
        left = av[r, 0:16, :].astype(F32)
        right = av[r, COLS - 16 : COLS, :].astype(F32)
        for q in range(2):
            stage[0, q * 8 + r : q * 8 + r + 1, :] = left[q : q + 1]
            stage[1, q * 8 + r : q * 8 + r + 1, :] = right[15 - q : 16 - q]
    bands[...] = stage[...].astype(BF16)
    gathered[0, f] = bands[...]

    def own(r):
        xp[r + 2, PAD : PAD + COLS, :] = av[r].astype(F32)

    loop(0, ROWS, own)

    pl.semaphore_wait(barrier, 2 + FACES + PLANE - 1 + DEPTH - 1)

    def copy(src, dst, send, recv, device):
        return pltpu.make_async_remote_copy(
            src_ref=src, dst_ref=dst, send_sem=send, recv_sem=recv, device_id=device, device_id_type=MESH
        )

    def seam_copy(src, dst, sends, recvs, k, j):
        device = ((f + j) % FACES, mirror if k else s)
        return copy(src, dst.at[k, f], sends.at[k * FACES + j], recvs.at[k * FACES + f], device)

    def seam_start(src, dst, sends, recvs):
        loop(1, FACES, lambda j: seam_copy(src, dst, sends, recvs, 0, j).start())
        loop(0, FACES, lambda j: seam_copy(src, dst, sends, recvs, 1, j).start())

    def seam_wait(src, dst, sends, recvs):
        def arrived(k, j):
            face = (f + j) % FACES
            copy(src, dst.at[k, face], sends.at[k * FACES + j], recvs.at[k * FACES + face], (face, s)).wait_recv()

        loop(1, FACES, lambda j: arrived(0, j))
        loop(0, FACES, lambda j: arrived(1, j))

    def seam_sent(src, dst, sends, recvs):
        loop(1, FACES, lambda j: seam_copy(src, dst, sends, recvs, 0, j).wait_send())
        loop(0, FACES, lambda j: seam_copy(src, dst, sends, recvs, 1, j).wait_send())

    def pick(src):
        out = []
        for e in range(2):
            sf, se, k = nb[0, 0, e, 0], nb[0, 0, e, 2], nb[0, 0, e, 3]
            picked[e] = src[k, sf, se].astype(F32)
            out.append([
                [jnp.where(k == 1, picked[e, q * 8 + 7 - r : q * 8 + 8 - r, :], picked[e, q * 8 + r : q * 8 + r + 1, :]) for r in range(ROWS)]
                for q in range(2)
            ])
        return out

    def beside(src, dst, n, device):
        return copy(src, dst, near_s.at[n], near_r.at[n], device)

    halos = [
        [beside(av.at[ROWS - 2 + t], halo.at[0, t], t, (f, down)) for t in range(2)],
        [beside(av.at[t], halo.at[1, t], 2 + t, (f, up)) for t in range(2)],
    ]
    corners = [beside(corner_out.at[0], corner_in.at[0], 4, (f, down)), beside(corner_out.at[1], corner_in.at[1], 5, (f, up))]
    grads = [
        beside(gb.at[pl.ds(ROWS - 2, 2)], ghalo.at[0], 6, (f, down)),
        beside(gb.at[pl.ds(0, 2)], ghalo.at[1], 7, (f, up)),
    ]
    gcorners = [beside(gcorner_out.at[0], gcorner_in.at[0], 8, (f, down)), beside(gcorner_out.at[1], gcorner_in.at[1], 9, (f, up))]

    seam_start(bands, gathered, seam_s, seam_r)
    for t in range(2):
        for side in range(2):
            halos[side][t].start()

    for c in little_in:
        c.wait()
    gain, scale = gain_ref[...], scale_ref[...]
    cw = cw_ref[...]
    wi_in.wait()
    wo_in.wait()
    prepare(wi[...], wo[...], scale, wd, wn)
    for c in cot_in:
        c.wait()

    def cells(pieces, size):
        forward(pieces, size, cw, gain, xp, cv, wi, wd, sc, nm, iv, hg, og, ig)

    def middle(r):
        cells([(r, c0) for c0 in range(64, COLS - 64, 64)], 64)

    def sides(rows):
        cells([(r, c0) for r in rows for c0 in (0, COLS - 64)], 64)

    inside = (jnp.where(s == 0, 0.0, 1.0), jnp.where(s == SLABS - 1, 0.0, 1.0))

    def fill(t):
        for side in range(2):
            halos[side][t].wait_recv()
            xp[t + side * (ROWS + 2), PAD : PAD + COLS, :] = halo[side, t].astype(F32) * inside[side]

    def seam_in():
        seam_wait(bands, gathered, seam_s, seam_r)
        strip = pick(gathered)
        for r in range(ROWS):
            for q in range(2):
                xp[r + 2, PAD - 1 - q : PAD - q, :] = strip[0][q][r]
                xp[r + 2, PAD + COLS + q : PAD + COLS + q + 1, :] = strip[1][q][r]
        for e in range(2):
            for q in range(2):
                for t in range(2):
                    place = e * 4 + q * 2 + t
                    corner_out[0, place : place + 1, :] = strip[e][q][ROWS - 2 + t]
                    corner_out[1, place : place + 1, :] = strip[e][q][t]
        for c in corners:
            c.start()

    def in_turn(n):
        @pl.when(n == 4)
        def _():
            fill(0)

        @pl.when(n == 6)
        def _():
            seam_in()
            fill(1)

        late = n // 4
        middle((1 - late) * (n + 2) + late * (n % 2 * 6 + n // 2 % 2))

    loop(0, ROWS, in_turn)
    sides((2, 3, 4, 5))

    for c in corners:
        c.wait_recv()
    for side in range(2):
        for t in range(2):
            row = t + side * (ROWS + 2)
            for q in range(2):
                left, right = q * 2 + t, 4 + q * 2 + t
                xp[row, PAD - 1 - q : PAD - q, :] = corner_in[side, left : left + 1, :] * inside[side]
                xp[row, PAD + COLS + q : PAD + COLS + q + 1, :] = corner_in[side, right : right + 1, :] * inside[side]
    sides((0, 1, 6, 7))

    products = og[...].T
    out_part = products * (0.5 * FACTOR * scale)
    in_part = ig[...] * FACTOR
    for b in range(HID // SHARE):
        big[b] = out_part[b * SHARE : (b + 1) * SHARE].astype(BF16)
    for b in range(HID // CH):
        for t in range(CH // SHARE):
            big[HID // SHARE + b * (CH // SHARE) + t] = in_part[t * SHARE : (t + 1) * SHARE, b * CH : (b + 1) * CH].astype(BF16)

    def plane_copy(src, dst, sends, recvs, j):
        other, device = in_plane(j)
        return copy(src(other), dst.at[a], sends.at[j], recvs.at[a], device)

    def plane_wait(dst, recvs, j):
        other, device = in_plane(j)
        copy(dst.at[other], dst.at[other], recvs.at[other], recvs.at[other], device).wait_recv()

    def depth_copy(src, dst, sends, recvs, j):
        other, device = in_depth(j)
        return copy(src, dst.at[z], sends.at[j], recvs.at[z], device)

    def depth_wait(dst, recvs, j):
        other, device = in_depth(j)
        copy(dst.at[other], dst.at[other], recvs.at[other], recvs.at[other], device).wait_recv()

    one = partial(plane_copy, lambda other: big.at[other], part1, one_s, one_r)
    two = partial(depth_copy, c2, part2, za_s, za_r)
    three = partial(plane_copy, lambda other: c3, part3, three_s, three_r)
    small_one = partial(depth_copy, small16, smallz, zb_s, zb_r)

    corner = x_lo * 2 + core

    def quad(j):
        other = (corner + j) % 4
        return copy(four, part4.at[corner], four_s.at[j], four_r.at[corner], (f, other // 2 * 16 + z * 2 + other % 2))

    def quad_wait(j):
        other = (corner + j) % 4
        copy(four, part4.at[other], four_s.at[j], four_r.at[other], (f, s)).wait_recv()

    def across(j):
        return copy(five, part5.at[f], five_s.at[j], five_r.at[f], ((f + j) % FACES, s))

    def across_wait(j):
        other = (f + j) % FACES
        copy(five, part5.at[other], five_s.at[j], five_r.at[other], (other, s)).wait_recv()

    loop(1, PLANE, lambda j: one(j).start())
    part1[a] = big[a]

    def send_grads(side):
        first = 0 if side else ROWS - 2
        for t in range(2):
            left = gp[first + t + 2, PAD : PAD + 8, :]
            right = gp[first + t + 2, PAD + COLS - 8 : PAD + COLS, :]
            for c in range(2):
                gcorner_out[side, c * 2 + t : c * 2 + t + 1, :] = left[c : c + 1]
                gcorner_out[side, 4 + c * 2 + t : 5 + c * 2 + t, :] = right[6 + c : 7 + c]
        gcorners[side].start()
        grads[side].start()

    def back_in_turn(n):
        late = n // 4
        backward((1 - late) * (n % 2 + n // 2 * 6) + late * (n - 2), gain, xp, wn, nm, iv, hg, ng, gp, gb, tg)

        @pl.when(n == 1)
        def _():
            send_grads(1)

        @pl.when(n == 3)
        def _():
            send_grads(0)

    loop(0, 6, back_in_turn)

    loop(1, PLANE, lambda j: plane_wait(part1, one_r, j))
    total = part1[0].astype(F32)
    for b in range(1, PLANE):
        total = total + part1[b].astype(F32)
    c2[...] = total.astype(BF16)
    part2[z] = c2[...]
    loop(1, DEPTH, lambda j: two(j).start())

    loop(6, ROWS, back_in_turn)

    small[...] = jnp.zeros_like(small)
    small[0:9, :] = jnp.sum(tg[...], 1) * FACTOR
    in_sum = jnp.sum((ig[...] * wi[...].astype(F32)).T, 0, keepdims=True)
    small[9:10, :] = in_sum / gain * FACTOR
    small[10:11, :] = jnp.sum(og[...].T * wo[...].astype(F32), 0, keepdims=True) * (0.5 * FACTOR)
    small16[...] = small[...].astype(BF16)
    smallz[z] = small16[...]
    loop(1, DEPTH, lambda j: small_one(j).start())

    for c in gcorners:
        c.wait_recv()
    for side in range(2):
        for t in range(2):
            row = t + side * (ROWS + 2)
            for c in range(2):
                left, right = c * 2 + t, 4 + c * 2 + t
                gp[row, PAD + c : PAD + c + 1, :] = gcorner_in[side, left : left + 1, :] * inside[side]
                gp[row, PAD + COLS - 2 + c : PAD + COLS - 1 + c, :] = gcorner_in[side, right : right + 1, :] * inside[side]
    for r in range(ROWS):
        left, right = jnp.zeros((8, CH), F32), jnp.zeros((8, CH), F32)
        for i in range(3):
            left = left + cw[3 * i : 3 * i + 1] * gp[r + 4 - 2 * i, PAD : PAD + 8, :]
            right = right + cw[3 * i + 2 : 3 * i + 3] * gp[r + 4 - 2 * i, PAD + COLS - 8 : PAD + COLS, :]
        for q in range(2):
            stage[0, q * 8 + r : q * 8 + r + 1, :] = left[1 - q : 2 - q]
            stage[1, q * 8 + r : q * 8 + r + 1, :] = right[6 + q : 7 + q]
    strips[...] = stage[...].astype(BF16)
    returned[0, f] = strips[...]
    seam_start(strips, returned, ret_s, ret_r)

    loop(1, DEPTH, lambda j: depth_wait(part2, za_r, j))
    c3[...] = jnp.sum(part2[...].astype(F32), 0).astype(BF16)
    loop(1, PLANE, lambda j: three(j).start())
    own_share = pltpu.make_async_copy(c3, part3.at[a], own_s.at[0])
    own_share.start()
    loop(1, DEPTH, lambda j: depth_wait(smallz, zb_r, j))
    four[...] = jnp.sum(smallz[...].astype(F32), 0).astype(BF16)
    part4[corner] = four[...]
    loop(1, 4, lambda j: quad(j).start())

    for side in range(2):
        grads[side].wait_recv()
        for t in range(2):
            gp[t + side * (ROWS + 2), PAD : PAD + COLS, :] = ghalo[side, t].astype(F32) * inside[side]

    def transposed_rows(low, high):
        loop(low, high, lambda r: transposed_row(r, cw, gp, cv, dxv, edge))

    transposed_rows(0, 4)

    loop(1, 4, quad_wait)
    five[...] = jnp.sum(part4[...].astype(F32), 0).astype(BF16)
    loop(1, FACES, lambda j: across(j).start())
    own_small = pltpu.make_async_copy(five, part5.at[f], own_s.at[1])
    own_small.start()
    transposed_rows(4, ROWS)

    seam_wait(strips, returned, ret_s, ret_r)
    back = pick(returned)
    for r in range(ROWS):
        for q in range(2):
            edge[0, r, q : q + 1, :] += back[0][q][r]
            edge[1, r, 15 - q : 16 - q, :] += back[1][q][r]
        dxv[r, 0:16, :] = edge[0, r].astype(BF16)
        dxv[r, COLS - 16 : COLS, :] = edge[1, r].astype(BF16)
    dx_out = [pltpu.make_async_copy(dxv.at[r], dx.at[0, r], dx_s.at[r]) for r in range(ROWS)]
    for c in dx_out:
        c.start()

    seam_sent(bands, gathered, seam_s, seam_r)
    seam_sent(strips, returned, ret_s, ret_r)
    for sent in halos[0] + halos[1] + corners + grads + gcorners:
        sent.wait_send()
    loop(1, PLANE, lambda j: one(j).wait_send())
    loop(1, DEPTH, lambda j: two(j).wait_send())
    loop(1, DEPTH, lambda j: small_one(j).wait_send())
    for c in dx_out:
        c.wait()
    own_share.wait()
    own_small.wait()
    loop(1, 4, lambda j: quad(j).wait_send())
    loop(1, PLANE, lambda j: three(j).wait_send())
    loop(1, FACES, lambda j: across(j).wait_send())
    loop(1, PLANE, lambda j: plane_wait(part3, three_r, j))
    loop(1, FACES, across_wait)


def finish(dx_in, parts, smalls, dx, o_conv, o_gain, o_in, o_out, o_scale, sem):
    moved = [pltpu.make_async_copy(dx_in.at[0, r], dx.at[0, r], sem.at[r]) for r in range(ROWS)]
    for c in moved:
        c.start()
    for b in range(HID // SHARE):
        o_out[b * SHARE : (b + 1) * SHARE, :] = parts[b].astype(F32)
    for b in range(HID // CH):
        for t in range(CH // SHARE):
            o_in[t * SHARE : (t + 1) * SHARE, b * CH : (b + 1) * CH] = parts[HID // SHARE + b * (CH // SHARE) + t].astype(F32)
    sums = jnp.sum(smalls[...].astype(F32), 0)
    o_conv[...] = sums[0:9]
    o_gain[...] = sums[9:10]
    o_scale[...] = sums[10:11]
    for c in moved:
        c.wait()


def body(activations, cotangent, conv_weight, norm_gain, w_in, w_out, layer_scale, neighbours):
    vmem = pl.BlockSpec(memory_space=pltpu.VMEM)
    anywhere = pl.BlockSpec(memory_space=pl.ANY)
    dma = pltpu.SemaphoreType.DMA

    def buf(*shape, dtype=F32):
        return pltpu.VMEM(shape, dtype)

    half = partial(buf, dtype=BF16)
    cells = jax.ShapeDtypeStruct((1, ROWS, COLS, CH), BF16)
    dx, parts, smalls = pl.pallas_call(
        kernel,
        out_shape=[half(1, ROWS, COLS, CH), half(PLANE, SHARE, CH), half(FACES, 16, CH)],
        in_specs=[anywhere] * 8,
        out_specs=[anywhere] * 3,
        scratch_shapes=[
            buf(9, CH), buf(1, CH), buf(1, CH), pltpu.SMEM((1, 1, 2, 4), jnp.int32),
            half(ROWS, COLS, CH), half(ROWS, COLS, CH), half(CH, HID), half(HID, CH), half(ROWS, COLS, CH),
            buf(ROWS + 4, WIDE, CH), buf(ROWS + 4, WIDE, CH), half(CH, HID), half(HID, CH),
            half(COLS, CH), buf(ROWS, COLS, CH), buf(ROWS, COLS, CH), half(ROWS, COLS, HID), buf(COLS, CH), half(ROWS, COLS, CH),
            buf(CH, HID), buf(CH, HID), buf(9, 8, CH), buf(2, ROWS, 16, CH),
            half(2, 16, CH), half(2, FACES, 2, 16, CH), buf(2, 16, CH), buf(2, 16, CH), buf(2, 8, CH), buf(2, 8, CH), buf(2, 8, CH), buf(2, 8, CH),
            half(2, 2, COLS, CH), half(2, 2, COLS, CH), half(2, 16, CH), half(2, FACES, 2, 16, CH),
            half(PLANE, SHARE, CH), buf(16, CH), half(16, CH), half(DEPTH, 16, CH), half(PLANE, SHARE, CH), half(SHARE, CH),
            half(DEPTH, SHARE, CH), half(SHARE, CH), half(16, CH), half(4, 16, CH), half(16, CH),
            dma((ROWS,)), dma((ROWS,)), dma((6,)), dma((ROWS,)), dma((2,)),
            dma((16,)), dma((16,)), dma((16,)), dma((16,)), dma((10,)), dma((10,)),
            dma((PLANE,)), dma((PLANE,)), dma((PLANE,)), dma((PLANE,)),
            dma((DEPTH,)), dma((DEPTH,)), dma((DEPTH,)), dma((DEPTH,)),
            dma((4,)), dma((4,)), dma((FACES,)), dma((FACES,)),
        ],
        compiler_params=pltpu.CompilerParams(collective_id=0, has_side_effects=True, vmem_limit_bytes=48 * 2**20),
    )(*[
        pltpu.with_memory_space_constraint(x, pltpu.HBM)
        for x in (activations, cotangent, conv_weight, norm_gain.reshape(1, CH), w_in, w_out, layer_scale.reshape(1, CH), neighbours)
    ])
    input_gradient, conv_grad, gain_grad, in_grad, out_grad, scale_grad = pl.pallas_call(
        finish,
        out_shape=[
            cells,
            jax.ShapeDtypeStruct((9, CH), F32),
            jax.ShapeDtypeStruct((1, CH), F32),
            jax.ShapeDtypeStruct((CH, HID), F32),
            jax.ShapeDtypeStruct((HID, CH), F32),
            jax.ShapeDtypeStruct((1, CH), F32),
        ],
        in_specs=[anywhere, vmem, vmem],
        out_specs=[anywhere] + [vmem] * 5,
        scratch_shapes=[dma((ROWS,))],
        compiler_params=pltpu.CompilerParams(vmem_limit_bytes=8 * 2**20),
    )(dx, parts, smalls)
    return input_gradient, conv_grad, gain_grad.reshape(CH), in_grad, out_grad, scale_grad.reshape(CH)


def solution(mesh):
    cells = P("face", "slab", None, None)
    return jax.shard_map(
        body,
        mesh=mesh,
        in_specs=(cells, cells, P(), P(), P(), P(), P(), cells),
        out_specs=(cells, P(), P(), P(), P(), P()),
        check_vma=False,
    )
```

```python
import math
from functools import partial

import jax
import jax.numpy as jnp
from jax import lax
from jax.experimental import pallas as pl
from jax.experimental.pallas import tpu as pltpu
from jax.sharding import PartitionSpec as P

F32, BF16 = jnp.float32, jnp.bfloat16
FACES, SLABS = 8, 32
DEPTH = 8
PLANE = 32
ROWS, COLS, CH, HID = 8, 512, 128, 512
PAD = 8
WIDE = COLS + 2 * PAD
CHUNK = 64
SHARE = 32
CELLS = FACES * SLABS * ROWS * COLS
FACTOR = float(CELLS) ** (-0.5)
EPSILON = 1e-6
SQRT_HALF = math.sqrt(0.5)
EXPONENT = -math.log2(math.e)
BIAS = math.log2(2 / math.sqrt(2 * math.pi))
MESH = pl.DeviceIdType.MESH


def dot(a, b, dims=((1,), (0,))):
    return lax.dot_general(a, b, (dims, ((), ())), preferred_element_type=F32)


def prepare(wi, wo, scale, wd_ref, wn_ref):
    wd_ref[...] = (wo.astype(F32) * (0.5 * scale)).T.astype(BF16)
    wn_ref[...] = wi.astype(F32).T.astype(BF16)


def forward(pieces, size, cw, gain, xp, cv, wi_ref, wd_ref, sc, nm, iv, hg, og, ig):
    total = len(pieces) * size
    for n, (r, c0) in enumerate(pieces):
        acc = None
        for i in range(3):
            for j in range(3):
                t = cw[3 * i + j : 3 * i + j + 1] * xp[r + 2 * i, pl.ds(PAD - 2 + 2 * j + c0, size), :]
                acc = t if acc is None else acc + t
        centred = acc - jnp.mean(acc, -1, keepdims=True)
        variance = jnp.mean(centred * centred, -1, keepdims=True)
        inverse = jnp.broadcast_to(lax.rsqrt(variance + EPSILON), (size, CH))
        normed = centred * inverse
        sc[n * size : (n + 1) * size, :] = (normed * gain).astype(BF16)
        nm[r, c0 : c0 + size, :] = normed
        iv[r, c0 : c0 + size, :] = inverse
    cot = jnp.concatenate([cv[r, c0 : c0 + size, :] for r, c0 in pieces], 0)
    scaled = sc[:total, :]
    hidden = dot(scaled, wi_ref[...])
    upstream = dot(cot, wd_ref[...])
    x = hidden * SQRT_HALF
    twice = 1.0 + lax.erf(x)
    activated = (hidden * twice).astype(BF16)
    density = jnp.exp2(x * x * EXPONENT + BIAS)
    hidden_grad = ((twice + hidden * density) * upstream).astype(BF16)
    for n, (r, c0) in enumerate(pieces):
        hg[r, c0 : c0 + size, :] = hidden_grad[n * size : (n + 1) * size]
    og[...] += dot(cot, activated, ((0,), (0,)))
    ig[...] += dot(scaled, hidden_grad, ((0,), (0,)))


def backward(r, gain, xp, wn_ref, nm, iv, hg, ng, gp, gb, tg):
    ng[...] = dot(hg[r], wn_ref[...])
    for c0 in range(0, COLS, CHUNK):
        d = ng[c0 : c0 + CHUNK, :] * gain
        normed = nm[r, c0 : c0 + CHUNK, :]
        d_mean = jnp.mean(d, -1, keepdims=True)
        dn_mean = jnp.mean(d * normed, -1, keepdims=True)
        gb16 = (iv[r, c0 : c0 + CHUNK, :] * (d - d_mean - normed * dn_mean)).astype(BF16)
        gb[r, c0 : c0 + CHUNK, :] = gb16
        g = gb16.astype(F32)
        gp[r + 2, PAD + c0 : PAD + c0 + CHUNK, :] = g
        for i in range(3):
            for j in range(3):
                t = g * xp[r + 2 * i, pl.ds(PAD - 2 + 2 * j + c0, CHUNK), :]
                tg[3 * i + j] += t.reshape(CHUNK // 8, 8, CH).sum(0)


def transposed_row(r, cw, gp, cv, dxv, edge):
    for c0 in range(0, COLS, CHUNK):
        acc = cv[r, c0 : c0 + CHUNK, :].astype(F32)
        for i in range(3):
            for j in range(3):
                acc = acc + cw[3 * i + j : 3 * i + j + 1] * gp[r + 4 - 2 * i, pl.ds(PAD + 2 - 2 * j + c0, CHUNK), :]
        dxv[r, c0 : c0 + CHUNK, :] = acc.astype(BF16)
        if c0 == 0:
            edge[0, r] = acc[:16]
        if c0 == COLS - CHUNK:
            edge[1, r] = acc[CHUNK - 16 :]


def kernel(
    act, cot, cw_hbm, gain_hbm, wi_hbm, wo_hbm, scale_hbm, nb_hbm,
    dx, part3, part5,
    cw_ref, gain_ref, scale_ref, nb, av, cv, wi, wo, dxv, xp, gp, wd, wn, sc, nm, iv, hg, ng, gb, og, ig, tg, edge, edge16,
    bands, gathered, stage, picked, corner_out, corner_in, gcorner_out, gcorner_in, halo, ghalo, strips, returned,
    big, small, small16, smallz, part1, c2, part2, c3, four, part4, five,
    act_s, cot_s, wgt_s, dx_s, own_s,
    seam_s, seam_r, ret_s, ret_r, near_s, near_r, one_s, one_r, three_s, three_r, za_s, za_r, zb_s, zb_r, four_s, four_r, five_s, five_r,
):
    f, s = lax.axis_index("face"), lax.axis_index("slab")
    x_lo, z, core = s // 16, (s // 2) % DEPTH, s % 2
    a = f * 4 + x_lo * 2 + core
    mirror = SLABS - 1 - s
    up, down = (s + SLABS - 1) % SLABS, (s + 1) % SLABS

    def in_plane(j):
        other = (a + j) % PLANE
        return other, (other // 4, ((other // 2) % 2) * 16 + z * 2 + other % 2)

    def in_depth(j):
        other = (z + j) % DEPTH
        return other, (f, x_lo * 16 + other * 2 + core)

    def loop(low, high, step):
        def body(j, carry):
            step(j)
            return carry

        lax.fori_loop(low, high, body, 0)

    act_in = [pltpu.make_async_copy(act.at[0, r], av.at[r], act_s.at[r]) for r in range(ROWS)]
    cot_in = [pltpu.make_async_copy(cot.at[0, r], cv.at[r], cot_s.at[r]) for r in range(ROWS)]
    wi_in = pltpu.make_async_copy(wi_hbm, wi, wgt_s.at[0])
    wo_in = pltpu.make_async_copy(wo_hbm, wo, wgt_s.at[1])
    little = [(nb_hbm, nb), (cw_hbm, cw_ref), (gain_hbm, gain_ref), (scale_hbm, scale_ref)]
    little_in = [pltpu.make_async_copy(src, dst, wgt_s.at[2 + n]) for n, (src, dst) in enumerate(little)]
    for c in act_in + little_in + [wi_in, wo_in] + cot_in:
        c.start()

    barrier = pltpu.get_barrier_semaphore()

    def greet(device):
        pl.semaphore_signal(barrier, inc=1, device_id=device, device_id_type=MESH)

    loop(0, FACES, lambda j: greet(((f + j) % FACES, mirror)))
    greet((f, up))
    greet((f, down))
    loop(1, PLANE, lambda j: greet(in_plane(j)[1]))
    loop(1, DEPTH, lambda j: greet(in_depth(j)[1]))

    og[...] = jnp.zeros_like(og)
    ig[...] = jnp.zeros_like(ig)
    tg[...] = jnp.zeros_like(tg)
    for r in range(ROWS + 4):
        gp[r, 0:PAD, :] = jnp.zeros((PAD, CH), F32)
        gp[r, PAD + COLS :, :] = jnp.zeros((PAD, CH), F32)
    for c in act_in:
        c.wait()
    for r in range(ROWS):
        left = av[r, 0:16, :].astype(F32)
        right = av[r, COLS - 16 : COLS, :].astype(F32)
        for q in range(2):
            stage[0, q * 8 + r : q * 8 + r + 1, :] = left[q : q + 1]
            stage[1, q * 8 + r : q * 8 + r + 1, :] = right[15 - q : 16 - q]
    bands[...] = stage[...].astype(BF16)
    gathered[0, f] = bands[...]

    def own(r):
        xp[r + 2, PAD : PAD + COLS, :] = av[r].astype(F32)

    loop(0, ROWS, own)

    pl.semaphore_wait(barrier, 2 + FACES + PLANE - 1 + DEPTH - 1)

    def copy(src, dst, send, recv, device):
        return pltpu.make_async_remote_copy(
            src_ref=src, dst_ref=dst, send_sem=send, recv_sem=recv, device_id=device, device_id_type=MESH
        )

    def seam_copy(src, dst, sends, recvs, k, j):
        device = ((f + j) % FACES, mirror if k else s)
        return copy(src, dst.at[k, f], sends.at[k * FACES + j], recvs.at[k * FACES + f], device)

    def seam_start(src, dst, sends, recvs):
        loop(1, FACES, lambda j: seam_copy(src, dst, sends, recvs, 0, j).start())
        loop(0, FACES, lambda j: seam_copy(src, dst, sends, recvs, 1, j).start())

    def seam_wait(src, dst, sends, recvs):
        def arrived(k, j):
            face = (f + j) % FACES
            copy(src, dst.at[k, face], sends.at[k * FACES + j], recvs.at[k * FACES + face], (face, s)).wait_recv()

        loop(1, FACES, lambda j: arrived(0, j))
        loop(0, FACES, lambda j: arrived(1, j))

    def seam_sent(src, dst, sends, recvs):
        loop(1, FACES, lambda j: seam_copy(src, dst, sends, recvs, 0, j).wait_send())
        loop(0, FACES, lambda j: seam_copy(src, dst, sends, recvs, 1, j).wait_send())

    def pick(src):
        out = []
        for e in range(2):
            sf, se, k = nb[0, 0, e, 0], nb[0, 0, e, 2], nb[0, 0, e, 3]
            picked[e] = src[k, sf, se].astype(F32)
            out.append([
                [jnp.where(k == 1, picked[e, q * 8 + 7 - r : q * 8 + 8 - r, :], picked[e, q * 8 + r : q * 8 + r + 1, :]) for r in range(ROWS)]
                for q in range(2)
            ])
        return out

    def beside(src, dst, n, device):
        return copy(src, dst, near_s.at[n], near_r.at[n], device)

    halos = [
        [beside(av.at[ROWS - 2 + t], halo.at[0, t], t, (f, down)) for t in range(2)],
        [beside(av.at[t], halo.at[1, t], 2 + t, (f, up)) for t in range(2)],
    ]
    corners = [beside(corner_out.at[0], corner_in.at[0], 4, (f, down)), beside(corner_out.at[1], corner_in.at[1], 5, (f, up))]
    grads = [
        beside(gb.at[pl.ds(ROWS - 2, 2)], ghalo.at[0], 6, (f, down)),
        beside(gb.at[pl.ds(0, 2)], ghalo.at[1], 7, (f, up)),
    ]
    gcorners = [beside(gcorner_out.at[0], gcorner_in.at[0], 8, (f, down)), beside(gcorner_out.at[1], gcorner_in.at[1], 9, (f, up))]

    for side in range(2):
        halos[side][0].start()
    seam_start(bands, gathered, seam_s, seam_r)
    for side in range(2):
        halos[side][1].start()

    for c in little_in:
        c.wait()
    gain, scale = gain_ref[...], scale_ref[...]
    cw = cw_ref[...]
    wi_in.wait()
    wo_in.wait()
    prepare(wi[...], wo[...], scale, wd, wn)
    for c in cot_in:
        c.wait()

    def cells(pieces, size):
        forward(pieces, size, cw, gain, xp, cv, wi, wd, sc, nm, iv, hg, og, ig)

    def middle(r):
        cells([(r, c0) for c0 in range(64, COLS - 64, 64)], 64)

    def sides(rows):
        cells([(r, c0) for r in rows for c0 in (0, COLS - 64)], 64)

    inside = (jnp.where(s == 0, 0.0, 1.0), jnp.where(s == SLABS - 1, 0.0, 1.0))

    def fill(t):
        for side in range(2):
            halos[side][t].wait_recv()
            xp[t + side * (ROWS + 2), PAD : PAD + COLS, :] = halo[side, t].astype(F32) * inside[side]

    def seam_in():
        seam_wait(bands, gathered, seam_s, seam_r)
        strip = pick(gathered)
        for r in range(ROWS):
            for q in range(2):
                xp[r + 2, PAD - 1 - q : PAD - q, :] = strip[0][q][r]
                xp[r + 2, PAD + COLS + q : PAD + COLS + q + 1, :] = strip[1][q][r]
        for e in range(2):
            for q in range(2):
                for t in range(2):
                    place = e * 4 + q * 2 + t
                    corner_out[0, place : place + 1, :] = strip[e][q][ROWS - 2 + t]
                    corner_out[1, place : place + 1, :] = strip[e][q][t]
        for c in corners:
            c.start()

    def in_turn(n):
        @pl.when(n == 4)
        def _():
            fill(0)

        @pl.when(n == 6)
        def _():
            seam_in()
            sides((2, 3, 4, 5))
            fill(1)

        late = n // 4
        middle((1 - late) * (n + 2) + late * (n % 2 * 6 + n // 2 % 2))

    loop(0, ROWS, in_turn)

    for c in corners:
        c.wait_recv()
    for side in range(2):
        for t in range(2):
            row = t + side * (ROWS + 2)
            for q in range(2):
                left, right = q * 2 + t, 4 + q * 2 + t
                xp[row, PAD - 1 - q : PAD - q, :] = corner_in[side, left : left + 1, :] * inside[side]
                xp[row, PAD + COLS + q : PAD + COLS + q + 1, :] = corner_in[side, right : right + 1, :] * inside[side]
    sides((0, 1, 6, 7))

    products = og[...].T
    out_part = products * (0.5 * FACTOR * scale)
    in_part = ig[...] * FACTOR
    for b in range(HID // SHARE):
        big[b] = out_part[b * SHARE : (b + 1) * SHARE].astype(BF16)
    for b in range(HID // CH):
        for t in range(CH // SHARE):
            big[HID // SHARE + b * (CH // SHARE) + t] = in_part[t * SHARE : (t + 1) * SHARE, b * CH : (b + 1) * CH].astype(BF16)

    def plane_copy(src, dst, sends, recvs, j):
        other, device = in_plane(j)
        return copy(src(other), dst.at[a], sends.at[j], recvs.at[a], device)

    def plane_wait(dst, recvs, j):
        other, device = in_plane(j)
        copy(dst.at[other], dst.at[other], recvs.at[other], recvs.at[other], device).wait_recv()

    def depth_copy(src, dst, sends, recvs, j):
        other, device = in_depth(j)
        return copy(src, dst.at[z], sends.at[j], recvs.at[z], device)

    def depth_wait(dst, recvs, j):
        other, device = in_depth(j)
        copy(dst.at[other], dst.at[other], recvs.at[other], recvs.at[other], device).wait_recv()

    one = partial(plane_copy, lambda other: big.at[other], part1, one_s, one_r)
    two = partial(depth_copy, c2, part2, za_s, za_r)
    three = partial(plane_copy, lambda other: c3, part3, three_s, three_r)
    small_one = partial(depth_copy, four, smallz, zb_s, zb_r)

    corner = x_lo * 2 + core

    def quad(j):
        other = (corner + j) % 4
        return copy(small16, part4.at[corner], four_s.at[j], four_r.at[corner], (f, other // 2 * 16 + z * 2 + other % 2))

    def quad_wait(j):
        other = (corner + j) % 4
        copy(small16, part4.at[other], four_s.at[j], four_r.at[other], (f, s)).wait_recv()

    def across(j):
        return copy(five, part5.at[f], five_s.at[j], five_r.at[f], ((f + j) % FACES, s))

    def across_wait(j):
        other = (f + j) % FACES
        copy(five, part5.at[other], five_s.at[j], five_r.at[other], (other, s)).wait_recv()

    loop(1, PLANE, lambda j: one(j).start())
    part1[a] = big[a]

    def send_grads(side):
        first = 0 if side else ROWS - 2
        for t in range(2):
            left = gp[first + t + 2, PAD : PAD + 8, :]
            right = gp[first + t + 2, PAD + COLS - 8 : PAD + COLS, :]
            for c in range(2):
                gcorner_out[side, c * 2 + t : c * 2 + t + 1, :] = left[c : c + 1]
                gcorner_out[side, 4 + c * 2 + t : 5 + c * 2 + t, :] = right[6 + c : 7 + c]
        gcorners[side].start()
        grads[side].start()

    def back_in_turn(n):
        late = n // 4
        backward((1 - late) * (n % 2 + n // 2 * 6) + late * (n - 2), gain, xp, wn, nm, iv, hg, ng, gp, gb, tg)

        @pl.when(n == 1)
        def _():
            send_grads(1)

        @pl.when(n == 3)
        def _():
            send_grads(0)

    loop(0, 6, back_in_turn)

    loop(1, PLANE, lambda j: plane_wait(part1, one_r, j))
    total = part1[0].astype(F32)
    for b in range(1, PLANE):
        total = total + part1[b].astype(F32)
    c2[...] = total.astype(BF16)
    part2[z] = c2[...]
    loop(1, DEPTH, lambda j: two(j).start())

    loop(6, ROWS, back_in_turn)

    small[...] = jnp.zeros_like(small)
    small[0:9, :] = jnp.sum(tg[...], 1) * FACTOR
    in_sum = jnp.sum((ig[...] * wi[...].astype(F32)).T, 0, keepdims=True)
    small[9:10, :] = in_sum / gain * FACTOR
    small[10:11, :] = jnp.sum(og[...].T * wo[...].astype(F32), 0, keepdims=True) * (0.5 * FACTOR)
    small16[...] = small[...].astype(BF16)
    part4[corner] = small16[...]
    loop(1, 4, lambda j: quad(j).start())

    for c in gcorners:
        c.wait_recv()
    for side in range(2):
        for t in range(2):
            row = t + side * (ROWS + 2)
            for c in range(2):
                left, right = c * 2 + t, 4 + c * 2 + t
                gp[row, PAD + c : PAD + c + 1, :] = gcorner_in[side, left : left + 1, :] * inside[side]
                gp[row, PAD + COLS - 2 + c : PAD + COLS - 1 + c, :] = gcorner_in[side, right : right + 1, :] * inside[side]
    for r in range(ROWS):
        left, right = jnp.zeros((8, CH), F32), jnp.zeros((8, CH), F32)
        for i in range(3):
            left = left + cw[3 * i : 3 * i + 1] * gp[r + 4 - 2 * i, PAD : PAD + 8, :]
            right = right + cw[3 * i + 2 : 3 * i + 3] * gp[r + 4 - 2 * i, PAD + COLS - 8 : PAD + COLS, :]
        for q in range(2):
            stage[0, q * 8 + r : q * 8 + r + 1, :] = left[1 - q : 2 - q]
            stage[1, q * 8 + r : q * 8 + r + 1, :] = right[6 + q : 7 + q]
    strips[...] = stage[...].astype(BF16)
    returned[0, f] = strips[...]
    seam_start(strips, returned, ret_s, ret_r)

    def dx_copy(r):
        inner = pl.ds(16, COLS - 32)
        return pltpu.make_async_copy(dxv.at[r, inner], dx.at[0, r, inner], dx_s.at[r])

    def transposed(r):
        transposed_row(r, cw, gp, cv, dxv, edge)
        dx_copy(r).start()

    loop(2, ROWS - 2, transposed)

    loop(1, 4, quad_wait)
    four[...] = jnp.sum(part4[...].astype(F32), 0).astype(BF16)
    smallz[z] = four[...]
    loop(1, DEPTH, lambda j: small_one(j).start())

    loop(1, DEPTH, lambda j: depth_wait(part2, za_r, j))
    c3[...] = jnp.sum(part2[...].astype(F32), 0).astype(BF16)
    loop(1, PLANE, lambda j: three(j).start())
    own_share = pltpu.make_async_copy(c3, part3.at[a], own_s.at[0])
    own_share.start()
    loop(1, DEPTH, lambda j: depth_wait(smallz, zb_r, j))
    five[...] = jnp.sum(smallz[...].astype(F32), 0).astype(BF16)
    loop(1, FACES, lambda j: across(j).start())
    own_small = pltpu.make_async_copy(five, part5.at[f], own_s.at[1])
    own_small.start()

    for side in range(2):
        grads[side].wait_recv()
        for t in range(2):
            gp[t + side * (ROWS + 2), PAD : PAD + COLS, :] = ghalo[side, t].astype(F32) * inside[side]

    loop(0, 4, lambda n: transposed(n % 2 + n // 2 * 6))

    seam_wait(strips, returned, ret_s, ret_r)
    back = pick(returned)
    for r in range(ROWS):
        for q in range(2):
            edge[0, r, q : q + 1, :] += back[0][q][r]
            edge[1, r, 15 - q : 16 - q, :] += back[1][q][r]
    edge16[...] = edge[...].astype(BF16)
    edge_out = [
        pltpu.make_async_copy(edge16.at[e], dx.at[0, :, pl.ds(e * (COLS - 16), 16)], dx_s.at[ROWS + e]) for e in range(2)
    ]
    for c in edge_out:
        c.start()

    seam_sent(bands, gathered, seam_s, seam_r)
    seam_sent(strips, returned, ret_s, ret_r)
    for sent in halos[0] + halos[1] + corners + grads + gcorners:
        sent.wait_send()
    loop(1, PLANE, lambda j: one(j).wait_send())
    loop(1, DEPTH, lambda j: two(j).wait_send())
    loop(1, DEPTH, lambda j: small_one(j).wait_send())
    loop(0, ROWS, lambda r: dx_copy(r).wait())
    for c in edge_out:
        c.wait()
    own_share.wait()
    own_small.wait()
    loop(1, 4, lambda j: quad(j).wait_send())
    loop(1, PLANE, lambda j: three(j).wait_send())
    loop(1, FACES, lambda j: across(j).wait_send())
    loop(1, PLANE, lambda j: plane_wait(part3, three_r, j))
    loop(1, FACES, across_wait)


def finish(dx_in, parts, smalls, dx, o_conv, o_gain, o_in, o_out, o_scale, sem):
    moved = [pltpu.make_async_copy(dx_in.at[0, r], dx.at[0, r], sem.at[r]) for r in range(ROWS)]
    for c in moved:
        c.start()
    for b in range(HID // SHARE):
        o_out[b * SHARE : (b + 1) * SHARE, :] = parts[b].astype(F32)
    for b in range(HID // CH):
        for t in range(CH // SHARE):
            o_in[t * SHARE : (t + 1) * SHARE, b * CH : (b + 1) * CH] = parts[HID // SHARE + b * (CH // SHARE) + t].astype(F32)
    sums = jnp.sum(smalls[...].astype(F32), 0)
    o_conv[...] = sums[0:9]
    o_gain[...] = sums[9:10]
    o_scale[...] = sums[10:11]
    for c in moved:
        c.wait()


def body(activations, cotangent, conv_weight, norm_gain, w_in, w_out, layer_scale, neighbours):
    vmem = pl.BlockSpec(memory_space=pltpu.VMEM)
    anywhere = pl.BlockSpec(memory_space=pl.ANY)
    dma = pltpu.SemaphoreType.DMA

    def buf(*shape, dtype=F32):
        return pltpu.VMEM(shape, dtype)

    half = partial(buf, dtype=BF16)
    cells = jax.ShapeDtypeStruct((1, ROWS, COLS, CH), BF16)
    dx, parts, smalls = pl.pallas_call(
        kernel,
        out_shape=[half(1, ROWS, COLS, CH), half(PLANE, SHARE, CH), half(FACES, 16, CH)],
        in_specs=[anywhere] * 8,
        out_specs=[anywhere] * 3,
        scratch_shapes=[
            buf(9, CH), buf(1, CH), buf(1, CH), pltpu.SMEM((1, 1, 2, 4), jnp.int32),
            half(ROWS, COLS, CH), half(ROWS, COLS, CH), half(CH, HID), half(HID, CH), half(ROWS, COLS, CH),
            buf(ROWS + 4, WIDE, CH), buf(ROWS + 4, WIDE, CH), half(CH, HID), half(HID, CH),
            half(COLS, CH), buf(ROWS, COLS, CH), buf(ROWS, COLS, CH), half(ROWS, COLS, HID), buf(COLS, CH), half(ROWS, COLS, CH),
            buf(CH, HID), buf(CH, HID), buf(9, 8, CH), buf(2, ROWS, 16, CH), half(2, ROWS, 16, CH),
            half(2, 16, CH), half(2, FACES, 2, 16, CH), buf(2, 16, CH), buf(2, 16, CH), buf(2, 8, CH), buf(2, 8, CH), buf(2, 8, CH), buf(2, 8, CH),
            half(2, 2, COLS, CH), half(2, 2, COLS, CH), half(2, 16, CH), half(2, FACES, 2, 16, CH),
            half(PLANE, SHARE, CH), buf(16, CH), half(16, CH), half(DEPTH, 16, CH), half(PLANE, SHARE, CH), half(SHARE, CH),
            half(DEPTH, SHARE, CH), half(SHARE, CH), half(16, CH), half(4, 16, CH), half(16, CH),
            dma((ROWS,)), dma((ROWS,)), dma((6,)), dma((ROWS + 2,)), dma((2,)),
            dma((16,)), dma((16,)), dma((16,)), dma((16,)), dma((10,)), dma((10,)),
            dma((PLANE,)), dma((PLANE,)), dma((PLANE,)), dma((PLANE,)),
            dma((DEPTH,)), dma((DEPTH,)), dma((DEPTH,)), dma((DEPTH,)),
            dma((4,)), dma((4,)), dma((FACES,)), dma((FACES,)),
        ],
        compiler_params=pltpu.CompilerParams(collective_id=0, has_side_effects=True, vmem_limit_bytes=48 * 2**20),
    )(*[
        pltpu.with_memory_space_constraint(x, pltpu.HBM)
        for x in (activations, cotangent, conv_weight, norm_gain.reshape(1, CH), w_in, w_out, layer_scale.reshape(1, CH), neighbours)
    ])
    input_gradient, conv_grad, gain_grad, in_grad, out_grad, scale_grad = pl.pallas_call(
        finish,
        out_shape=[
            cells,
            jax.ShapeDtypeStruct((9, CH), F32),
            jax.ShapeDtypeStruct((1, CH), F32),
            jax.ShapeDtypeStruct((CH, HID), F32),
            jax.ShapeDtypeStruct((HID, CH), F32),
            jax.ShapeDtypeStruct((1, CH), F32),
        ],
        in_specs=[anywhere, vmem, vmem],
        out_specs=[anywhere] + [vmem] * 5,
        scratch_shapes=[dma((ROWS,))],
        compiler_params=pltpu.CompilerParams(vmem_limit_bytes=8 * 2**20),
    )(dx, parts, smalls)
    return input_gradient, conv_grad, gain_grad.reshape(CH), in_grad, out_grad, scale_grad.reshape(CH)


def solution(mesh):
    cells = P("face", "slab", None, None)
    return jax.shard_map(
        body,
        mesh=mesh,
        in_specs=(cells, cells, P(), P(), P(), P(), P(), cells),
        out_specs=(cells, P(), P(), P(), P(), P()),
        check_vma=False,
    )
```

```python
import math
from functools import partial

import jax
import jax.numpy as jnp
from jax import lax
from jax.experimental import pallas as pl
from jax.experimental.pallas import tpu as pltpu
from jax.sharding import PartitionSpec as P

F32, BF16 = jnp.float32, jnp.bfloat16
FACES, SLABS = 8, 32
DEPTH = 8
PLANE = 32
ROWS, COLS, CH, HID = 8, 512, 128, 512
PAD = 8
WIDE = COLS + 2 * PAD
CHUNK = 64
SHARE = 32
CELLS = FACES * SLABS * ROWS * COLS
FACTOR = float(CELLS) ** (-0.5)
EPSILON = 1e-6
SQRT_HALF = math.sqrt(0.5)
EXPONENT = -math.log2(math.e)
BIAS = math.log2(2 / math.sqrt(2 * math.pi))
MESH = pl.DeviceIdType.MESH


def dot(a, b, dims=((1,), (0,))):
    return lax.dot_general(a, b, (dims, ((), ())), preferred_element_type=F32)


def prepare(wi, wo, scale, wd_ref, wn_ref):
    wd_ref[...] = (wo.astype(F32) * (0.5 * scale)).T.astype(BF16)
    wn_ref[...] = wi.astype(F32).T.astype(BF16)


def forward(pieces, size, cw, gain, xp, cv, wi_ref, wd_ref, sc, nm, iv, hg, og, ig):
    total = len(pieces) * size
    for n, (r, c0) in enumerate(pieces):
        acc = None
        for i in range(3):
            for j in range(3):
                t = cw[3 * i + j : 3 * i + j + 1] * xp[r + 2 * i, pl.ds(PAD - 2 + 2 * j + c0, size), :]
                acc = t if acc is None else acc + t
        centred = acc - jnp.mean(acc, -1, keepdims=True)
        variance = jnp.mean(centred * centred, -1, keepdims=True)
        inverse = jnp.broadcast_to(lax.rsqrt(variance + EPSILON), (size, CH))
        normed = centred * inverse
        sc[n * size : (n + 1) * size, :] = (normed * gain).astype(BF16)
        nm[r, c0 : c0 + size, :] = normed
        iv[r, c0 : c0 + size, :] = inverse
    cot = jnp.concatenate([cv[r, c0 : c0 + size, :] for r, c0 in pieces], 0)
    scaled = sc[:total, :]
    hidden = dot(scaled, wi_ref[...])
    upstream = dot(cot, wd_ref[...])
    x = hidden * SQRT_HALF
    twice = 1.0 + lax.erf(x)
    activated = (hidden * twice).astype(BF16)
    density = jnp.exp2(x * x * EXPONENT + BIAS)
    hidden_grad = ((twice + hidden * density) * upstream).astype(BF16)
    for n, (r, c0) in enumerate(pieces):
        hg[r, c0 : c0 + size, :] = hidden_grad[n * size : (n + 1) * size]
    og[...] += dot(cot, activated, ((0,), (0,)))
    ig[...] += dot(scaled, hidden_grad, ((0,), (0,)))


def backward(r, gain, xp, wn_ref, nm, iv, hg, ng, gp, gb, tg):
    ng[...] = dot(hg[r], wn_ref[...])
    for c0 in range(0, COLS, CHUNK):
        d = ng[c0 : c0 + CHUNK, :] * gain
        normed = nm[r, c0 : c0 + CHUNK, :]
        d_mean = jnp.mean(d, -1, keepdims=True)
        dn_mean = jnp.mean(d * normed, -1, keepdims=True)
        gb16 = (iv[r, c0 : c0 + CHUNK, :] * (d - d_mean - normed * dn_mean)).astype(BF16)
        gb[r, c0 : c0 + CHUNK, :] = gb16
        g = gb16.astype(F32)
        gp[r + 2, PAD + c0 : PAD + c0 + CHUNK, :] = g
        for i in range(3):
            for j in range(3):
                t = g * xp[r + 2 * i, pl.ds(PAD - 2 + 2 * j + c0, CHUNK), :]
                tg[3 * i + j] += t.reshape(CHUNK // 8, 8, CH).sum(0)


def transposed_row(r, cw, gp, cv, dxv, edge):
    for c0 in range(0, COLS, CHUNK):
        acc = cv[r, c0 : c0 + CHUNK, :].astype(F32)
        for i in range(3):
            for j in range(3):
                acc = acc + cw[3 * i + j : 3 * i + j + 1] * gp[r + 4 - 2 * i, pl.ds(PAD + 2 - 2 * j + c0, CHUNK), :]
        dxv[r, c0 : c0 + CHUNK, :] = acc.astype(BF16)
        if c0 == 0:
            edge[0, r] = acc[:16]
        if c0 == COLS - CHUNK:
            edge[1, r] = acc[CHUNK - 16 :]


def kernel(
    act, cot, cw_hbm, gain_hbm, wi_hbm, wo_hbm, scale_hbm, nb_hbm,
    dx, part3, part5,
    cw_ref, gain_ref, scale_ref, nb, av, cv, wi, wo, dxv, xp, gp, wd, wn, sc, nm, iv, hg, ng, gb, og, ig, tg, edge, edge16,
    bands, gathered, stage, picked, corner_out, corner_in, gcorner_out, gcorner_in, halo, ghalo, strips, returned,
    big, small, small16, smallz, part1, c2, part2, c3, four, part4, five,
    act_s, cot_s, wgt_s, dx_s, own_s,
    seam_s, seam_r, ret_s, ret_r, near_s, near_r, one_s, one_r, three_s, three_r, za_s, za_r, zb_s, zb_r, four_s, four_r, five_s, five_r,
):
    f, s = lax.axis_index("face"), lax.axis_index("slab")
    x_lo, z, core = s // 16, (s // 2) % DEPTH, s % 2
    a = f * 4 + x_lo * 2 + core
    mirror = SLABS - 1 - s
    up, down = (s + SLABS - 1) % SLABS, (s + 1) % SLABS

    def in_plane(j):
        other = (a + j) % PLANE
        return other, (other // 4, ((other // 2) % 2) * 16 + z * 2 + other % 2)

    def in_depth(j):
        other = (z + j) % DEPTH
        return other, (f, x_lo * 16 + other * 2 + core)

    def loop(low, high, step):
        def body(j, carry):
            step(j)
            return carry

        lax.fori_loop(low, high, body, 0)

    act_in = [pltpu.make_async_copy(act.at[0, r], av.at[r], act_s.at[r]) for r in range(ROWS)]
    cot_in = [pltpu.make_async_copy(cot.at[0, r], cv.at[r], cot_s.at[r]) for r in range(ROWS)]
    wi_in = pltpu.make_async_copy(wi_hbm, wi, wgt_s.at[0])
    wo_in = pltpu.make_async_copy(wo_hbm, wo, wgt_s.at[1])
    little = [(nb_hbm, nb), (cw_hbm, cw_ref), (gain_hbm, gain_ref), (scale_hbm, scale_ref)]
    little_in = [pltpu.make_async_copy(src, dst, wgt_s.at[2 + n]) for n, (src, dst) in enumerate(little)]
    for c in act_in + little_in + [wi_in, wo_in] + cot_in:
        c.start()

    barrier = pltpu.get_barrier_semaphore()

    def greet(device):
        pl.semaphore_signal(barrier, inc=1, device_id=device, device_id_type=MESH)

    loop(0, FACES, lambda j: greet(((f + j) % FACES, mirror)))
    greet((f, up))
    greet((f, down))
    loop(1, PLANE, lambda j: greet(in_plane(j)[1]))
    loop(1, DEPTH, lambda j: greet(in_depth(j)[1]))

    og[...] = jnp.zeros_like(og)
    ig[...] = jnp.zeros_like(ig)
    tg[...] = jnp.zeros_like(tg)
    for r in range(ROWS + 4):
        gp[r, 0:PAD, :] = jnp.zeros((PAD, CH), F32)
        gp[r, PAD + COLS :, :] = jnp.zeros((PAD, CH), F32)
    for c in act_in:
        c.wait()
    for r in range(ROWS):
        left = av[r, 0:16, :].astype(F32)
        right = av[r, COLS - 16 : COLS, :].astype(F32)
        for q in range(2):
            stage[0, q * 8 + r : q * 8 + r + 1, :] = left[q : q + 1]
            stage[1, q * 8 + r : q * 8 + r + 1, :] = right[15 - q : 16 - q]
    bands[...] = stage[...].astype(BF16)
    gathered[0, f] = bands[...]

    def own(r):
        xp[r + 2, PAD : PAD + COLS, :] = av[r].astype(F32)

    loop(0, ROWS, own)

    pl.semaphore_wait(barrier, 2 + FACES + PLANE - 1 + DEPTH - 1)

    def copy(src, dst, send, recv, device):
        return pltpu.make_async_remote_copy(
            src_ref=src, dst_ref=dst, send_sem=send, recv_sem=recv, device_id=device, device_id_type=MESH
        )

    def seam_copy(src, dst, sends, recvs, k, j):
        device = ((f + j) % FACES, mirror if k else s)
        return copy(src, dst.at[k, f], sends.at[k * FACES + j], recvs.at[k * FACES + f], device)

    def seam_start(src, dst, sends, recvs):
        loop(1, FACES, lambda j: seam_copy(src, dst, sends, recvs, 0, j).start())
        loop(0, FACES, lambda j: seam_copy(src, dst, sends, recvs, 1, j).start())

    def seam_wait(src, dst, sends, recvs):
        def arrived(k, j):
            face = (f + j) % FACES
            copy(src, dst.at[k, face], sends.at[k * FACES + j], recvs.at[k * FACES + face], (face, s)).wait_recv()

        loop(1, FACES, lambda j: arrived(0, j))
        loop(0, FACES, lambda j: arrived(1, j))

    def seam_sent(src, dst, sends, recvs):
        loop(1, FACES, lambda j: seam_copy(src, dst, sends, recvs, 0, j).wait_send())
        loop(0, FACES, lambda j: seam_copy(src, dst, sends, recvs, 1, j).wait_send())

    def pick(src):
        out = []
        for e in range(2):
            sf, se, k = nb[0, 0, e, 0], nb[0, 0, e, 2], nb[0, 0, e, 3]
            picked[e] = src[k, sf, se].astype(F32)
            out.append([
                [jnp.where(k == 1, picked[e, q * 8 + 7 - r : q * 8 + 8 - r, :], picked[e, q * 8 + r : q * 8 + r + 1, :]) for r in range(ROWS)]
                for q in range(2)
            ])
        return out

    def beside(src, dst, n, device):
        return copy(src, dst, near_s.at[n], near_r.at[n], device)

    halos = [
        [beside(av.at[ROWS - 2 + t], halo.at[0, t], t, (f, down)) for t in range(2)],
        [beside(av.at[t], halo.at[1, t], 2 + t, (f, up)) for t in range(2)],
    ]
    corners = [beside(corner_out.at[0], corner_in.at[0], 4, (f, down)), beside(corner_out.at[1], corner_in.at[1], 5, (f, up))]
    grads = [
        beside(gb.at[pl.ds(ROWS - 2, 2)], ghalo.at[0], 6, (f, down)),
        beside(gb.at[pl.ds(0, 2)], ghalo.at[1], 7, (f, up)),
    ]
    gcorners = [beside(gcorner_out.at[0], gcorner_in.at[0], 8, (f, down)), beside(gcorner_out.at[1], gcorner_in.at[1], 9, (f, up))]

    for side in range(2):
        halos[side][0].start()
    seam_start(bands, gathered, seam_s, seam_r)
    for side in range(2):
        halos[side][1].start()

    for c in little_in:
        c.wait()
    gain, scale = gain_ref[...], scale_ref[...]
    cw = cw_ref[...]
    wi_in.wait()
    wo_in.wait()
    prepare(wi[...], wo[...], scale, wd, wn)
    for c in cot_in:
        c.wait()

    def cells(pieces, size):
        forward(pieces, size, cw, gain, xp, cv, wi, wd, sc, nm, iv, hg, og, ig)

    def middle(r):
        cells([(r, c0) for c0 in range(64, COLS - 64, 64)], 64)

    def sides(rows):
        cells([(r, c0) for r in rows for c0 in (0, COLS - 64)], 64)

    inside = (jnp.where(s == 0, 0.0, 1.0), jnp.where(s == SLABS - 1, 0.0, 1.0))

    def fill(t):
        for side in range(2):
            halos[side][t].wait_recv()
            xp[t + side * (ROWS + 2), PAD : PAD + COLS, :] = halo[side, t].astype(F32) * inside[side]

    def seam_in():
        seam_wait(bands, gathered, seam_s, seam_r)
        strip = pick(gathered)
        for r in range(ROWS):
            for q in range(2):
                xp[r + 2, PAD - 1 - q : PAD - q, :] = strip[0][q][r]
                xp[r + 2, PAD + COLS + q : PAD + COLS + q + 1, :] = strip[1][q][r]
        for e in range(2):
            for q in range(2):
                for t in range(2):
                    place = e * 4 + q * 2 + t
                    corner_out[0, place : place + 1, :] = strip[e][q][ROWS - 2 + t]
                    corner_out[1, place : place + 1, :] = strip[e][q][t]
        for c in corners:
            c.start()

    def in_turn(n):
        @pl.when(n == 4)
        def _():
            fill(0)

        @pl.when(n == 6)
        def _():
            seam_in()
            sides((2, 3, 4, 5))
            fill(1)

        late = n // 4
        middle((1 - late) * (n + 2) + late * (n % 2 * 6 + n // 2 % 2))

    loop(0, ROWS, in_turn)

    for c in corners:
        c.wait_recv()
    for side in range(2):
        for t in range(2):
            row = t + side * (ROWS + 2)
            for q in range(2):
                left, right = q * 2 + t, 4 + q * 2 + t
                xp[row, PAD - 1 - q : PAD - q, :] = corner_in[side, left : left + 1, :] * inside[side]
                xp[row, PAD + COLS + q : PAD + COLS + q + 1, :] = corner_in[side, right : right + 1, :] * inside[side]
    sides((0, 1, 6, 7))

    products = og[...].T
    out_part = products * (0.5 * FACTOR * scale)
    in_part = ig[...] * FACTOR
    for b in range(HID // SHARE):
        big[b] = out_part[b * SHARE : (b + 1) * SHARE].astype(BF16)
    for b in range(HID // CH):
        for t in range(CH // SHARE):
            big[HID // SHARE + b * (CH // SHARE) + t] = in_part[t * SHARE : (t + 1) * SHARE, b * CH : (b + 1) * CH].astype(BF16)

    def plane_copy(src, dst, sends, recvs, j):
        other, device = in_plane(j)
        return copy(src(other), dst.at[a], sends.at[j], recvs.at[a], device)

    def plane_wait(dst, recvs, j):
        other, device = in_plane(j)
        copy(dst.at[other], dst.at[other], recvs.at[other], recvs.at[other], device).wait_recv()

    def depth_copy(src, dst, sends, recvs, j):
        other, device = in_depth(j)
        return copy(src, dst.at[z], sends.at[j], recvs.at[z], device)

    def depth_wait(dst, recvs, j):
        other, device = in_depth(j)
        copy(dst.at[other], dst.at[other], recvs.at[other], recvs.at[other], device).wait_recv()

    one = partial(plane_copy, lambda other: big.at[other], part1, one_s, one_r)
    two = partial(depth_copy, c2, part2, za_s, za_r)
    three = partial(plane_copy, lambda other: c3, part3, three_s, three_r)
    small_one = partial(depth_copy, four, smallz, zb_s, zb_r)

    corner = x_lo * 2 + core

    def quad(j):
        other = (corner + j) % 4
        return copy(small16, part4.at[corner], four_s.at[j], four_r.at[corner], (f, other // 2 * 16 + z * 2 + other % 2))

    def quad_wait(j):
        other = (corner + j) % 4
        copy(small16, part4.at[other], four_s.at[j], four_r.at[other], (f, s)).wait_recv()

    def across(j):
        return copy(five, part5.at[f], five_s.at[j], five_r.at[f], ((f + j) % FACES, s))

    def across_wait(j):
        other = (f + j) % FACES
        copy(five, part5.at[other], five_s.at[j], five_r.at[other], (other, s)).wait_recv()

    loop(1, PLANE, lambda j: one(j).start())
    part1[a] = big[a]

    def send_grads(side):
        first = 0 if side else ROWS - 2
        for t in range(2):
            left = gp[first + t + 2, PAD : PAD + 8, :]
            right = gp[first + t + 2, PAD + COLS - 8 : PAD + COLS, :]
            for c in range(2):
                gcorner_out[side, c * 2 + t : c * 2 + t + 1, :] = left[c : c + 1]
                gcorner_out[side, 4 + c * 2 + t : 5 + c * 2 + t, :] = right[6 + c : 7 + c]
        gcorners[side].start()
        grads[side].start()

    def back_in_turn(n):
        late = n // 4
        backward((1 - late) * (n % 2 + n // 2 * 6) + late * (n - 2), gain, xp, wn, nm, iv, hg, ng, gp, gb, tg)

        @pl.when(n == 1)
        def _():
            send_grads(1)

        @pl.when(n == 3)
        def _():
            send_grads(0)

    loop(0, ROWS, back_in_turn)

    small[...] = jnp.zeros_like(small)
    small[0:9, :] = jnp.sum(tg[...], 1) * FACTOR
    in_sum = jnp.sum((ig[...] * wi[...].astype(F32)).T, 0, keepdims=True)
    small[9:10, :] = in_sum / gain * FACTOR
    small[10:11, :] = jnp.sum(og[...].T * wo[...].astype(F32), 0, keepdims=True) * (0.5 * FACTOR)
    small16[...] = small[...].astype(BF16)
    part4[corner] = small16[...]
    loop(1, 4, lambda j: quad(j).start())

    loop(1, PLANE, lambda j: plane_wait(part1, one_r, j))
    total = part1[0].astype(F32)
    for b in range(1, PLANE):
        total = total + part1[b].astype(F32)
    c2[...] = total.astype(BF16)
    part2[z] = c2[...]
    loop(1, DEPTH, lambda j: two(j).start())

    loop(1, 4, quad_wait)
    four[...] = jnp.sum(part4[...].astype(F32), 0).astype(BF16)
    smallz[z] = four[...]
    loop(1, DEPTH, lambda j: small_one(j).start())

    for c in gcorners:
        c.wait_recv()
    for side in range(2):
        for t in range(2):
            row = t + side * (ROWS + 2)
            for c in range(2):
                left, right = c * 2 + t, 4 + c * 2 + t
                gp[row, PAD + c : PAD + c + 1, :] = gcorner_in[side, left : left + 1, :] * inside[side]
                gp[row, PAD + COLS - 2 + c : PAD + COLS - 1 + c, :] = gcorner_in[side, right : right + 1, :] * inside[side]
    for r in range(ROWS):
        left, right = jnp.zeros((8, CH), F32), jnp.zeros((8, CH), F32)
        for i in range(3):
            left = left + cw[3 * i : 3 * i + 1] * gp[r + 4 - 2 * i, PAD : PAD + 8, :]
            right = right + cw[3 * i + 2 : 3 * i + 3] * gp[r + 4 - 2 * i, PAD + COLS - 8 : PAD + COLS, :]
        for q in range(2):
            stage[0, q * 8 + r : q * 8 + r + 1, :] = left[1 - q : 2 - q]
            stage[1, q * 8 + r : q * 8 + r + 1, :] = right[6 + q : 7 + q]
    strips[...] = stage[...].astype(BF16)
    returned[0, f] = strips[...]
    seam_start(strips, returned, ret_s, ret_r)

    def dx_copy(r):
        inner = pl.ds(16, COLS - 32)
        return pltpu.make_async_copy(dxv.at[r, inner], dx.at[0, r, inner], dx_s.at[r])

    def transposed(r):
        transposed_row(r, cw, gp, cv, dxv, edge)
        dx_copy(r).start()

    loop(2, ROWS - 2, transposed)

    loop(1, DEPTH, lambda j: depth_wait(part2, za_r, j))
    c3[...] = jnp.sum(part2[...].astype(F32), 0).astype(BF16)
    loop(1, PLANE, lambda j: three(j).start())
    own_share = pltpu.make_async_copy(c3, part3.at[a], own_s.at[0])
    own_share.start()
    loop(1, DEPTH, lambda j: depth_wait(smallz, zb_r, j))
    five[...] = jnp.sum(smallz[...].astype(F32), 0).astype(BF16)
    loop(1, FACES, lambda j: across(j).start())
    own_small = pltpu.make_async_copy(five, part5.at[f], own_s.at[1])
    own_small.start()

    for side in range(2):
        grads[side].wait_recv()
        for t in range(2):
            gp[t + side * (ROWS + 2), PAD : PAD + COLS, :] = ghalo[side, t].astype(F32) * inside[side]

    loop(0, 4, lambda n: transposed(n % 2 + n // 2 * 6))

    seam_wait(strips, returned, ret_s, ret_r)
    back = pick(returned)
    for r in range(ROWS):
        for q in range(2):
            edge[0, r, q : q + 1, :] += back[0][q][r]
            edge[1, r, 15 - q : 16 - q, :] += back[1][q][r]
    edge16[...] = edge[...].astype(BF16)
    edge_out = [
        pltpu.make_async_copy(edge16.at[e], dx.at[0, :, pl.ds(e * (COLS - 16), 16)], dx_s.at[ROWS + e]) for e in range(2)
    ]
    for c in edge_out:
        c.start()

    seam_sent(bands, gathered, seam_s, seam_r)
    seam_sent(strips, returned, ret_s, ret_r)
    for sent in halos[0] + halos[1] + corners + grads + gcorners:
        sent.wait_send()
    loop(1, PLANE, lambda j: one(j).wait_send())
    loop(1, DEPTH, lambda j: two(j).wait_send())
    loop(1, DEPTH, lambda j: small_one(j).wait_send())
    loop(0, ROWS, lambda r: dx_copy(r).wait())
    for c in edge_out:
        c.wait()
    own_share.wait()
    own_small.wait()
    loop(1, 4, lambda j: quad(j).wait_send())
    loop(1, PLANE, lambda j: three(j).wait_send())
    loop(1, FACES, lambda j: across(j).wait_send())
    loop(1, PLANE, lambda j: plane_wait(part3, three_r, j))
    loop(1, FACES, across_wait)


def finish(dx_in, parts, smalls, dx, o_conv, o_gain, o_in, o_out, o_scale, sem):
    moved = [pltpu.make_async_copy(dx_in.at[0, r], dx.at[0, r], sem.at[r]) for r in range(ROWS)]
    for c in moved:
        c.start()
    for b in range(HID // SHARE):
        o_out[b * SHARE : (b + 1) * SHARE, :] = parts[b].astype(F32)
    for b in range(HID // CH):
        for t in range(CH // SHARE):
            o_in[t * SHARE : (t + 1) * SHARE, b * CH : (b + 1) * CH] = parts[HID // SHARE + b * (CH // SHARE) + t].astype(F32)
    sums = jnp.sum(smalls[...].astype(F32), 0)
    o_conv[...] = sums[0:9]
    o_gain[...] = sums[9:10]
    o_scale[...] = sums[10:11]
    for c in moved:
        c.wait()


def body(activations, cotangent, conv_weight, norm_gain, w_in, w_out, layer_scale, neighbours):
    vmem = pl.BlockSpec(memory_space=pltpu.VMEM)
    anywhere = pl.BlockSpec(memory_space=pl.ANY)
    dma = pltpu.SemaphoreType.DMA

    def buf(*shape, dtype=F32):
        return pltpu.VMEM(shape, dtype)

    half = partial(buf, dtype=BF16)
    cells = jax.ShapeDtypeStruct((1, ROWS, COLS, CH), BF16)
    dx, parts, smalls = pl.pallas_call(
        kernel,
        out_shape=[half(1, ROWS, COLS, CH), half(PLANE, SHARE, CH), half(FACES, 16, CH)],
        in_specs=[anywhere] * 8,
        out_specs=[anywhere] * 3,
        scratch_shapes=[
            buf(9, CH), buf(1, CH), buf(1, CH), pltpu.SMEM((1, 1, 2, 4), jnp.int32),
            half(ROWS, COLS, CH), half(ROWS, COLS, CH), half(CH, HID), half(HID, CH), half(ROWS, COLS, CH),
            buf(ROWS + 4, WIDE, CH), buf(ROWS + 4, WIDE, CH), half(CH, HID), half(HID, CH),
            half(COLS, CH), buf(ROWS, COLS, CH), buf(ROWS, COLS, CH), half(ROWS, COLS, HID), buf(COLS, CH), half(ROWS, COLS, CH),
            buf(CH, HID), buf(CH, HID), buf(9, 8, CH), buf(2, ROWS, 16, CH), half(2, ROWS, 16, CH),
            half(2, 16, CH), half(2, FACES, 2, 16, CH), buf(2, 16, CH), buf(2, 16, CH), buf(2, 8, CH), buf(2, 8, CH), buf(2, 8, CH), buf(2, 8, CH),
            half(2, 2, COLS, CH), half(2, 2, COLS, CH), half(2, 16, CH), half(2, FACES, 2, 16, CH),
            half(PLANE, SHARE, CH), buf(16, CH), half(16, CH), half(DEPTH, 16, CH), half(PLANE, SHARE, CH), half(SHARE, CH),
            half(DEPTH, SHARE, CH), half(SHARE, CH), half(16, CH), half(4, 16, CH), half(16, CH),
            dma((ROWS,)), dma((ROWS,)), dma((6,)), dma((ROWS + 2,)), dma((2,)),
            dma((16,)), dma((16,)), dma((16,)), dma((16,)), dma((10,)), dma((10,)),
            dma((PLANE,)), dma((PLANE,)), dma((PLANE,)), dma((PLANE,)),
            dma((DEPTH,)), dma((DEPTH,)), dma((DEPTH,)), dma((DEPTH,)),
            dma((4,)), dma((4,)), dma((FACES,)), dma((FACES,)),
        ],
        compiler_params=pltpu.CompilerParams(collective_id=0, has_side_effects=True, vmem_limit_bytes=48 * 2**20),
    )(*[
        pltpu.with_memory_space_constraint(x, pltpu.HBM)
        for x in (activations, cotangent, conv_weight, norm_gain.reshape(1, CH), w_in, w_out, layer_scale.reshape(1, CH), neighbours)
    ])
    input_gradient, conv_grad, gain_grad, in_grad, out_grad, scale_grad = pl.pallas_call(
        finish,
        out_shape=[
            cells,
            jax.ShapeDtypeStruct((9, CH), F32),
            jax.ShapeDtypeStruct((1, CH), F32),
            jax.ShapeDtypeStruct((CH, HID), F32),
            jax.ShapeDtypeStruct((HID, CH), F32),
            jax.ShapeDtypeStruct((1, CH), F32),
        ],
        in_specs=[anywhere, vmem, vmem],
        out_specs=[anywhere] + [vmem] * 5,
        scratch_shapes=[dma((ROWS,))],
        compiler_params=pltpu.CompilerParams(vmem_limit_bytes=8 * 2**20),
    )(dx, parts, smalls)
    return input_gradient, conv_grad, gain_grad.reshape(CH), in_grad, out_grad, scale_grad.reshape(CH)


def solution(mesh):
    cells = P("face", "slab", None, None)
    return jax.shard_map(
        body,
        mesh=mesh,
        in_specs=(cells, cells, P(), P(), P(), P(), P(), cells),
        out_specs=(cells, P(), P(), P(), P(), P()),
        check_vma=False,
    )
```

```python
import math
from functools import partial

import jax
import jax.numpy as jnp
from jax import lax
from jax.experimental import pallas as pl
from jax.experimental.pallas import tpu as pltpu
from jax.sharding import PartitionSpec as P

F32, BF16 = jnp.float32, jnp.bfloat16
FACES, SLABS = 8, 32
DEPTH = 8
PLANE = 32
ROWS, COLS, CH, HID = 8, 512, 128, 512
PAD = 8
WIDE = COLS + 2 * PAD
CHUNK = 64
SHARE = 32
CELLS = FACES * SLABS * ROWS * COLS
FACTOR = float(CELLS) ** (-0.5)
EPSILON = 1e-6
SQRT_HALF = math.sqrt(0.5)
EXPONENT = -math.log2(math.e)
BIAS = math.log2(2 / math.sqrt(2 * math.pi))
MESH = pl.DeviceIdType.MESH


def dot(a, b, dims=((1,), (0,))):
    return lax.dot_general(a, b, (dims, ((), ())), preferred_element_type=F32)


def prepare(wi, wo, scale, wd_ref, wn_ref):
    wd_ref[...] = (wo.astype(F32) * (0.5 * scale)).T.astype(BF16)
    wn_ref[...] = wi.astype(F32).T.astype(BF16)


def forward(pieces, size, cw, gain, xp, cv, wi_ref, wd_ref, sc, nm, iv, hg, og, ig):
    total = len(pieces) * size
    for n, (r, c0) in enumerate(pieces):
        acc = None
        for i in range(3):
            for j in range(3):
                t = cw[3 * i + j : 3 * i + j + 1] * xp[r + 2 * i, pl.ds(PAD - 2 + 2 * j + c0, size), :]
                acc = t if acc is None else acc + t
        centred = acc - jnp.mean(acc, -1, keepdims=True)
        variance = jnp.mean(centred * centred, -1, keepdims=True)
        inverse = jnp.broadcast_to(lax.rsqrt(variance + EPSILON), (size, CH))
        normed = centred * inverse
        sc[n * size : (n + 1) * size, :] = (normed * gain).astype(BF16)
        nm[r, c0 : c0 + size, :] = normed
        iv[r, c0 : c0 + size, :] = inverse
    cot = jnp.concatenate([cv[r, c0 : c0 + size, :] for r, c0 in pieces], 0)
    scaled = sc[:total, :]
    hidden = dot(scaled, wi_ref[...])
    upstream = dot(cot, wd_ref[...])
    x = hidden * SQRT_HALF
    twice = 1.0 + lax.erf(x)
    activated = (hidden * twice).astype(BF16)
    density = jnp.exp2(x * x * EXPONENT + BIAS)
    hidden_grad = ((twice + hidden * density) * upstream).astype(BF16)
    for n, (r, c0) in enumerate(pieces):
        hg[r, c0 : c0 + size, :] = hidden_grad[n * size : (n + 1) * size]
    og[...] += dot(cot, activated, ((0,), (0,)))
    ig[...] += dot(scaled, hidden_grad, ((0,), (0,)))


def backward(r, gain, xp, wn_ref, nm, iv, hg, ng, gp, gb, tg):
    ng[...] = dot(hg[r], wn_ref[...])
    for c0 in range(0, COLS, CHUNK):
        d = ng[c0 : c0 + CHUNK, :] * gain
        normed = nm[r, c0 : c0 + CHUNK, :]
        d_mean = jnp.mean(d, -1, keepdims=True)
        dn_mean = jnp.mean(d * normed, -1, keepdims=True)
        gb16 = (iv[r, c0 : c0 + CHUNK, :] * (d - d_mean - normed * dn_mean)).astype(BF16)
        gb[r, c0 : c0 + CHUNK, :] = gb16
        g = gb16.astype(F32)
        gp[r + 2, PAD + c0 : PAD + c0 + CHUNK, :] = g
        for i in range(3):
            for j in range(3):
                t = g * xp[r + 2 * i, pl.ds(PAD - 2 + 2 * j + c0, CHUNK), :]
                tg[3 * i + j] += t.reshape(CHUNK // 8, 8, CH).sum(0)


def transposed_row(r, cw, gp, cv, dxv, edge):
    for c0 in range(0, COLS, CHUNK):
        acc = cv[r, c0 : c0 + CHUNK, :].astype(F32)
        for i in range(3):
            for j in range(3):
                acc = acc + cw[3 * i + j : 3 * i + j + 1] * gp[r + 4 - 2 * i, pl.ds(PAD + 2 - 2 * j + c0, CHUNK), :]
        dxv[r, c0 : c0 + CHUNK, :] = acc.astype(BF16)
        if c0 == 0:
            edge[0, r] = acc[:16]
        if c0 == COLS - CHUNK:
            edge[1, r] = acc[CHUNK - 16 :]


def kernel(
    act, cot, cw_hbm, gain_hbm, wi_hbm, wo_hbm, scale_hbm, nb_hbm,
    dx, part3, part5,
    cw_ref, gain_ref, scale_ref, nb, av, cv, wi, wo, dxv, xp, gp, wd, wn, sc, nm, iv, hg, ng, gb, og, ig, tg, edge, edge16,
    bands, gathered, stage, picked, corner_out, corner_in, gcorner_out, gcorner_in, halo, ghalo, strips, returned,
    big, small, small16, smallz, part1, c2, part2, c3, four, part4, five,
    act_s, cot_s, wgt_s, dx_s, own_s,
    seam_s, seam_r, ret_s, ret_r, near_s, near_r, one_s, one_r, three_s, three_r, za_s, za_r, zb_s, zb_r, four_s, four_r, five_s, five_r,
):
    f, s = lax.axis_index("face"), lax.axis_index("slab")
    x_lo, z, core = s // 16, (s // 2) % DEPTH, s % 2
    a = f * 4 + x_lo * 2 + core
    mirror = SLABS - 1 - s
    up, down = (s + SLABS - 1) % SLABS, (s + 1) % SLABS

    def in_plane(j):
        other = (a + j) % PLANE
        return other, (other // 4, ((other // 2) % 2) * 16 + z * 2 + other % 2)

    def in_depth(j):
        other = (z + j) % DEPTH
        return other, (f, x_lo * 16 + other * 2 + core)

    def loop(low, high, step):
        def body(j, carry):
            step(j)
            return carry

        lax.fori_loop(low, high, body, 0)

    act_in = [pltpu.make_async_copy(act.at[0, r], av.at[r], act_s.at[r]) for r in range(ROWS)]
    cot_in = [pltpu.make_async_copy(cot.at[0, r], cv.at[r], cot_s.at[r]) for r in range(ROWS)]
    wi_in = pltpu.make_async_copy(wi_hbm, wi, wgt_s.at[0])
    wo_in = pltpu.make_async_copy(wo_hbm, wo, wgt_s.at[1])
    little = [(nb_hbm, nb), (cw_hbm, cw_ref), (gain_hbm, gain_ref), (scale_hbm, scale_ref)]
    little_in = [pltpu.make_async_copy(src, dst, wgt_s.at[2 + n]) for n, (src, dst) in enumerate(little)]
    for c in act_in + little_in + [wi_in, wo_in] + cot_in:
        c.start()

    barrier = pltpu.get_barrier_semaphore()

    def greet(device):
        pl.semaphore_signal(barrier, inc=1, device_id=device, device_id_type=MESH)

    loop(0, FACES, lambda j: greet(((f + j) % FACES, mirror)))
    greet((f, up))
    greet((f, down))
    loop(1, PLANE, lambda j: greet(in_plane(j)[1]))
    loop(1, DEPTH, lambda j: greet(in_depth(j)[1]))

    og[...] = jnp.zeros_like(og)
    ig[...] = jnp.zeros_like(ig)
    tg[...] = jnp.zeros_like(tg)
    for r in range(ROWS + 4):
        gp[r, 0:PAD, :] = jnp.zeros((PAD, CH), F32)
        gp[r, PAD + COLS :, :] = jnp.zeros((PAD, CH), F32)
    for c in act_in:
        c.wait()
    for r in range(ROWS):
        left = av[r, 0:16, :].astype(F32)
        right = av[r, COLS - 16 : COLS, :].astype(F32)
        for q in range(2):
            stage[0, q * 8 + r : q * 8 + r + 1, :] = left[q : q + 1]
            stage[1, q * 8 + r : q * 8 + r + 1, :] = right[15 - q : 16 - q]
    bands[...] = stage[...].astype(BF16)
    gathered[0, f] = bands[...]

    def own(r):
        xp[r + 2, PAD : PAD + COLS, :] = av[r].astype(F32)

    loop(0, ROWS, own)

    pl.semaphore_wait(barrier, 2 + FACES + PLANE - 1 + DEPTH - 1)

    def copy(src, dst, send, recv, device):
        return pltpu.make_async_remote_copy(
            src_ref=src, dst_ref=dst, send_sem=send, recv_sem=recv, device_id=device, device_id_type=MESH
        )

    def seam_copy(src, dst, sends, recvs, k, j):
        device = ((f + j) % FACES, mirror if k else s)
        return copy(src, dst.at[k, f], sends.at[k * FACES + j], recvs.at[k * FACES + f], device)

    def seam_start(src, dst, sends, recvs):
        loop(1, FACES, lambda j: seam_copy(src, dst, sends, recvs, 0, j).start())
        loop(0, FACES, lambda j: seam_copy(src, dst, sends, recvs, 1, j).start())

    def seam_wait(src, dst, sends, recvs):
        def arrived(k, j):
            face = (f + j) % FACES
            copy(src, dst.at[k, face], sends.at[k * FACES + j], recvs.at[k * FACES + face], (face, s)).wait_recv()

        loop(1, FACES, lambda j: arrived(0, j))
        loop(0, FACES, lambda j: arrived(1, j))

    def seam_sent(src, dst, sends, recvs):
        loop(1, FACES, lambda j: seam_copy(src, dst, sends, recvs, 0, j).wait_send())
        loop(0, FACES, lambda j: seam_copy(src, dst, sends, recvs, 1, j).wait_send())

    def pick(src):
        out = []
        for e in range(2):
            sf, se, k = nb[0, 0, e, 0], nb[0, 0, e, 2], nb[0, 0, e, 3]
            picked[e] = src[k, sf, se].astype(F32)
            out.append([
                [jnp.where(k == 1, picked[e, q * 8 + 7 - r : q * 8 + 8 - r, :], picked[e, q * 8 + r : q * 8 + r + 1, :]) for r in range(ROWS)]
                for q in range(2)
            ])
        return out

    def beside(src, dst, n, device):
        return copy(src, dst, near_s.at[n], near_r.at[n], device)

    halos = [
        [beside(av.at[ROWS - 2 + t], halo.at[0, t], t, (f, down)) for t in range(2)],
        [beside(av.at[t], halo.at[1, t], 2 + t, (f, up)) for t in range(2)],
    ]
    corners = [beside(corner_out.at[0], corner_in.at[0], 4, (f, down)), beside(corner_out.at[1], corner_in.at[1], 5, (f, up))]
    grads = [
        beside(gb.at[pl.ds(ROWS - 2, 2)], ghalo.at[0], 6, (f, down)),
        beside(gb.at[pl.ds(0, 2)], ghalo.at[1], 7, (f, up)),
    ]
    gcorners = [beside(gcorner_out.at[0], gcorner_in.at[0], 8, (f, down)), beside(gcorner_out.at[1], gcorner_in.at[1], 9, (f, up))]

    seam_start(bands, gathered, seam_s, seam_r)
    for side in range(2):
        halos[side][0].start()
    for side in range(2):
        halos[side][1].start()

    for c in little_in:
        c.wait()
    gain, scale = gain_ref[...], scale_ref[...]
    cw = cw_ref[...]
    wi_in.wait()
    wo_in.wait()
    prepare(wi[...], wo[...], scale, wd, wn)
    for c in cot_in:
        c.wait()

    def cells(pieces, size):
        forward(pieces, size, cw, gain, xp, cv, wi, wd, sc, nm, iv, hg, og, ig)

    def middle(r):
        cells([(r, c0) for c0 in range(64, COLS - 64, 64)], 64)

    def sides(rows):
        cells([(r, c0) for r in rows for c0 in (0, COLS - 64)], 64)

    inside = (jnp.where(s == 0, 0.0, 1.0), jnp.where(s == SLABS - 1, 0.0, 1.0))

    def fill(t):
        for side in range(2):
            halos[side][t].wait_recv()
            xp[t + side * (ROWS + 2), PAD : PAD + COLS, :] = halo[side, t].astype(F32) * inside[side]

    def seam_in():
        seam_wait(bands, gathered, seam_s, seam_r)
        strip = pick(gathered)
        for r in range(ROWS):
            for q in range(2):
                xp[r + 2, PAD - 1 - q : PAD - q, :] = strip[0][q][r]
                xp[r + 2, PAD + COLS + q : PAD + COLS + q + 1, :] = strip[1][q][r]
        for e in range(2):
            for q in range(2):
                for t in range(2):
                    place = e * 4 + q * 2 + t
                    corner_out[0, place : place + 1, :] = strip[e][q][ROWS - 2 + t]
                    corner_out[1, place : place + 1, :] = strip[e][q][t]
        for c in corners:
            c.start()

    def in_turn(n):
        @pl.when(n == 4)
        def _():
            fill(0)

        @pl.when(n == 6)
        def _():
            seam_in()
            sides((2, 3, 4, 5))
            fill(1)

        late = n // 4
        middle((1 - late) * (n + 2) + late * (n % 2 * 6 + n // 2 % 2))

    loop(0, ROWS, in_turn)

    for c in corners:
        c.wait_recv()
    for side in range(2):
        for t in range(2):
            row = t + side * (ROWS + 2)
            for q in range(2):
                left, right = q * 2 + t, 4 + q * 2 + t
                xp[row, PAD - 1 - q : PAD - q, :] = corner_in[side, left : left + 1, :] * inside[side]
                xp[row, PAD + COLS + q : PAD + COLS + q + 1, :] = corner_in[side, right : right + 1, :] * inside[side]
    sides((0, 1, 6, 7))

    products = og[...].T
    out_part = products * (0.5 * FACTOR * scale)
    in_part = ig[...] * FACTOR
    for b in range(HID // SHARE):
        big[b] = out_part[b * SHARE : (b + 1) * SHARE].astype(BF16)
    for b in range(HID // CH):
        for t in range(CH // SHARE):
            big[HID // SHARE + b * (CH // SHARE) + t] = in_part[t * SHARE : (t + 1) * SHARE, b * CH : (b + 1) * CH].astype(BF16)

    def plane_copy(src, dst, sends, recvs, j):
        other, device = in_plane(j)
        return copy(src(other), dst.at[a], sends.at[j], recvs.at[a], device)

    def plane_wait(dst, recvs, j):
        other, device = in_plane(j)
        copy(dst.at[other], dst.at[other], recvs.at[other], recvs.at[other], device).wait_recv()

    def depth_copy(src, dst, sends, recvs, j):
        other, device = in_depth(j)
        return copy(src, dst.at[z], sends.at[j], recvs.at[z], device)

    def depth_wait(dst, recvs, j):
        other, device = in_depth(j)
        copy(dst.at[other], dst.at[other], recvs.at[other], recvs.at[other], device).wait_recv()

    one = partial(plane_copy, lambda other: big.at[other], part1, one_s, one_r)
    two = partial(depth_copy, c2, part2, za_s, za_r)
    three = partial(plane_copy, lambda other: c3, part3, three_s, three_r)
    small_one = partial(depth_copy, four, smallz, zb_s, zb_r)

    corner = x_lo * 2 + core

    def quad(j):
        other = (corner + j) % 4
        return copy(small16, part4.at[corner], four_s.at[j], four_r.at[corner], (f, other // 2 * 16 + z * 2 + other % 2))

    def quad_wait(j):
        other = (corner + j) % 4
        copy(small16, part4.at[other], four_s.at[j], four_r.at[other], (f, s)).wait_recv()

    def across(j):
        return copy(five, part5.at[f], five_s.at[j], five_r.at[f], ((f + j) % FACES, s))

    def across_wait(j):
        other = (f + j) % FACES
        copy(five, part5.at[other], five_s.at[j], five_r.at[other], (other, s)).wait_recv()

    loop(1, PLANE, lambda j: one(j).start())
    part1[a] = big[a]

    def send_grads(side):
        first = 0 if side else ROWS - 2
        for t in range(2):
            left = gp[first + t + 2, PAD : PAD + 8, :]
            right = gp[first + t + 2, PAD + COLS - 8 : PAD + COLS, :]
            for c in range(2):
                gcorner_out[side, c * 2 + t : c * 2 + t + 1, :] = left[c : c + 1]
                gcorner_out[side, 4 + c * 2 + t : 5 + c * 2 + t, :] = right[6 + c : 7 + c]
        gcorners[side].start()
        grads[side].start()

    def back_in_turn(n):
        late = n // 4
        backward((1 - late) * (n % 2 + n // 2 * 6) + late * (n - 2), gain, xp, wn, nm, iv, hg, ng, gp, gb, tg)

        @pl.when(n == 1)
        def _():
            send_grads(1)

        @pl.when(n == 3)
        def _():
            send_grads(0)

    loop(0, ROWS, back_in_turn)

    small[...] = jnp.zeros_like(small)
    small[0:9, :] = jnp.sum(tg[...], 1) * FACTOR
    in_sum = jnp.sum((ig[...] * wi[...].astype(F32)).T, 0, keepdims=True)
    small[9:10, :] = in_sum / gain * FACTOR
    small[10:11, :] = jnp.sum(og[...].T * wo[...].astype(F32), 0, keepdims=True) * (0.5 * FACTOR)
    small16[...] = small[...].astype(BF16)
    part4[corner] = small16[...]
    loop(1, 4, lambda j: quad(j).start())

    loop(1, PLANE, lambda j: plane_wait(part1, one_r, j))
    total = part1[0].astype(F32)
    for b in range(1, PLANE):
        total = total + part1[b].astype(F32)
    c2[...] = total.astype(BF16)
    part2[z] = c2[...]
    loop(1, DEPTH, lambda j: two(j).start())

    loop(1, 4, quad_wait)
    four[...] = jnp.sum(part4[...].astype(F32), 0).astype(BF16)
    smallz[z] = four[...]
    loop(1, DEPTH, lambda j: small_one(j).start())

    for c in gcorners:
        c.wait_recv()
    for side in range(2):
        for t in range(2):
            row = t + side * (ROWS + 2)
            for c in range(2):
                left, right = c * 2 + t, 4 + c * 2 + t
                gp[row, PAD + c : PAD + c + 1, :] = gcorner_in[side, left : left + 1, :] * inside[side]
                gp[row, PAD + COLS - 2 + c : PAD + COLS - 1 + c, :] = gcorner_in[side, right : right + 1, :] * inside[side]
    for r in range(ROWS):
        left, right = jnp.zeros((8, CH), F32), jnp.zeros((8, CH), F32)
        for i in range(3):
            left = left + cw[3 * i : 3 * i + 1] * gp[r + 4 - 2 * i, PAD : PAD + 8, :]
            right = right + cw[3 * i + 2 : 3 * i + 3] * gp[r + 4 - 2 * i, PAD + COLS - 8 : PAD + COLS, :]
        for q in range(2):
            stage[0, q * 8 + r : q * 8 + r + 1, :] = left[1 - q : 2 - q]
            stage[1, q * 8 + r : q * 8 + r + 1, :] = right[6 + q : 7 + q]
    strips[...] = stage[...].astype(BF16)
    returned[0, f] = strips[...]
    seam_start(strips, returned, ret_s, ret_r)

    def dx_copy(r):
        inner = pl.ds(16, COLS - 32)
        return pltpu.make_async_copy(dxv.at[r, inner], dx.at[0, r, inner], dx_s.at[r])

    def transposed(r):
        transposed_row(r, cw, gp, cv, dxv, edge)
        dx_copy(r).start()

    loop(2, ROWS - 2, transposed)

    loop(1, DEPTH, lambda j: depth_wait(part2, za_r, j))
    c3[...] = jnp.sum(part2[...].astype(F32), 0).astype(BF16)
    loop(1, PLANE, lambda j: three(j).start())
    own_share = pltpu.make_async_copy(c3, part3.at[a], own_s.at[0])
    own_share.start()
    loop(1, DEPTH, lambda j: depth_wait(smallz, zb_r, j))
    five[...] = jnp.sum(smallz[...].astype(F32), 0).astype(BF16)
    loop(1, FACES, lambda j: across(j).start())
    own_small = pltpu.make_async_copy(five, part5.at[f], own_s.at[1])
    own_small.start()

    for side in range(2):
        grads[side].wait_recv()
        for t in range(2):
            gp[t + side * (ROWS + 2), PAD : PAD + COLS, :] = ghalo[side, t].astype(F32) * inside[side]

    loop(0, 4, lambda n: transposed(n % 2 + n // 2 * 6))

    seam_wait(strips, returned, ret_s, ret_r)
    back = pick(returned)
    for r in range(ROWS):
        for q in range(2):
            edge[0, r, q : q + 1, :] += back[0][q][r]
            edge[1, r, 15 - q : 16 - q, :] += back[1][q][r]
    edge16[...] = edge[...].astype(BF16)
    edge_out = [
        pltpu.make_async_copy(edge16.at[e], dx.at[0, :, pl.ds(e * (COLS - 16), 16)], dx_s.at[ROWS + e]) for e in range(2)
    ]
    for c in edge_out:
        c.start()

    seam_sent(bands, gathered, seam_s, seam_r)
    seam_sent(strips, returned, ret_s, ret_r)
    for sent in halos[0] + halos[1] + corners + grads + gcorners:
        sent.wait_send()
    loop(1, PLANE, lambda j: one(j).wait_send())
    loop(1, DEPTH, lambda j: two(j).wait_send())
    loop(1, DEPTH, lambda j: small_one(j).wait_send())
    loop(0, ROWS, lambda r: dx_copy(r).wait())
    for c in edge_out:
        c.wait()
    own_share.wait()
    own_small.wait()
    loop(1, 4, lambda j: quad(j).wait_send())
    loop(1, PLANE, lambda j: three(j).wait_send())
    loop(1, FACES, lambda j: across(j).wait_send())
    loop(1, PLANE, lambda j: plane_wait(part3, three_r, j))
    loop(1, FACES, across_wait)


def finish(dx_in, parts, smalls, dx, o_conv, o_gain, o_in, o_out, o_scale, sem):
    moved = [pltpu.make_async_copy(dx_in.at[0, r], dx.at[0, r], sem.at[r]) for r in range(ROWS)]
    for c in moved:
        c.start()
    for b in range(HID // SHARE):
        o_out[b * SHARE : (b + 1) * SHARE, :] = parts[b].astype(F32)
    for b in range(HID // CH):
        for t in range(CH // SHARE):
            o_in[t * SHARE : (t + 1) * SHARE, b * CH : (b + 1) * CH] = parts[HID // SHARE + b * (CH // SHARE) + t].astype(F32)
    sums = jnp.sum(smalls[...].astype(F32), 0)
    o_conv[...] = sums[0:9]
    o_gain[...] = sums[9:10]
    o_scale[...] = sums[10:11]
    for c in moved:
        c.wait()


def body(activations, cotangent, conv_weight, norm_gain, w_in, w_out, layer_scale, neighbours):
    vmem = pl.BlockSpec(memory_space=pltpu.VMEM)
    anywhere = pl.BlockSpec(memory_space=pl.ANY)
    dma = pltpu.SemaphoreType.DMA

    def buf(*shape, dtype=F32):
        return pltpu.VMEM(shape, dtype)

    half = partial(buf, dtype=BF16)
    cells = jax.ShapeDtypeStruct((1, ROWS, COLS, CH), BF16)
    dx, parts, smalls = pl.pallas_call(
        kernel,
        out_shape=[half(1, ROWS, COLS, CH), half(PLANE, SHARE, CH), half(FACES, 16, CH)],
        in_specs=[anywhere] * 8,
        out_specs=[anywhere] * 3,
        scratch_shapes=[
            buf(9, CH), buf(1, CH), buf(1, CH), pltpu.SMEM((1, 1, 2, 4), jnp.int32),
            half(ROWS, COLS, CH), half(ROWS, COLS, CH), half(CH, HID), half(HID, CH), half(ROWS, COLS, CH),
            buf(ROWS + 4, WIDE, CH), buf(ROWS + 4, WIDE, CH), half(CH, HID), half(HID, CH),
            half(COLS, CH), buf(ROWS, COLS, CH), buf(ROWS, COLS, CH), half(ROWS, COLS, HID), buf(COLS, CH), half(ROWS, COLS, CH),
            buf(CH, HID), buf(CH, HID), buf(9, 8, CH), buf(2, ROWS, 16, CH), half(2, ROWS, 16, CH),
            half(2, 16, CH), half(2, FACES, 2, 16, CH), buf(2, 16, CH), buf(2, 16, CH), buf(2, 8, CH), buf(2, 8, CH), buf(2, 8, CH), buf(2, 8, CH),
            half(2, 2, COLS, CH), half(2, 2, COLS, CH), half(2, 16, CH), half(2, FACES, 2, 16, CH),
            half(PLANE, SHARE, CH), buf(16, CH), half(16, CH), half(DEPTH, 16, CH), half(PLANE, SHARE, CH), half(SHARE, CH),
            half(DEPTH, SHARE, CH), half(SHARE, CH), half(16, CH), half(4, 16, CH), half(16, CH),
            dma((ROWS,)), dma((ROWS,)), dma((6,)), dma((ROWS + 2,)), dma((2,)),
            dma((16,)), dma((16,)), dma((16,)), dma((16,)), dma((10,)), dma((10,)),
            dma((PLANE,)), dma((PLANE,)), dma((PLANE,)), dma((PLANE,)),
            dma((DEPTH,)), dma((DEPTH,)), dma((DEPTH,)), dma((DEPTH,)),
            dma((4,)), dma((4,)), dma((FACES,)), dma((FACES,)),
        ],
        compiler_params=pltpu.CompilerParams(collective_id=0, has_side_effects=True, vmem_limit_bytes=48 * 2**20),
    )(*[
        pltpu.with_memory_space_constraint(x, pltpu.HBM)
        for x in (activations, cotangent, conv_weight, norm_gain.reshape(1, CH), w_in, w_out, layer_scale.reshape(1, CH), neighbours)
    ])
    input_gradient, conv_grad, gain_grad, in_grad, out_grad, scale_grad = pl.pallas_call(
        finish,
        out_shape=[
            cells,
            jax.ShapeDtypeStruct((9, CH), F32),
            jax.ShapeDtypeStruct((1, CH), F32),
            jax.ShapeDtypeStruct((CH, HID), F32),
            jax.ShapeDtypeStruct((HID, CH), F32),
            jax.ShapeDtypeStruct((1, CH), F32),
        ],
        in_specs=[anywhere, vmem, vmem],
        out_specs=[anywhere] + [vmem] * 5,
        scratch_shapes=[dma((ROWS,))],
        compiler_params=pltpu.CompilerParams(vmem_limit_bytes=8 * 2**20),
    )(dx, parts, smalls)
    return input_gradient, conv_grad, gain_grad.reshape(CH), in_grad, out_grad, scale_grad.reshape(CH)


def solution(mesh):
    cells = P("face", "slab", None, None)
    return jax.shard_map(
        body,
        mesh=mesh,
        in_specs=(cells, cells, P(), P(), P(), P(), P(), cells),
        out_specs=(cells, P(), P(), P(), P(), P()),
        check_vma=False,
    )
```
